128 devices in a mesh: row: 8 (over z_lo, y), col: 4 (over x), ch: 4 (over z_hi, core).
Axes of the slice: x: 4, y: 4, z: 4 (z_hi: 2, z_lo: 2; z = z_hi * 2 + z_lo), core: 2. Of those that a mesh axis runs over, the one named last changes fastest.
Arguments:
- pair: bfloat16 [960, 960, 128], P(('row', 'ch'), 'col'), may hold values from -400 to 400
- norm_gain: float32 [128], replicated, may hold values from 0.25 to 1.75
- norm_shift: float32 [128], replicated, may hold values from -3 to 3
- proj_weight: bfloat16 [128, 4, 128], replicated, may hold values from -0.5 to 0.5
- proj_bias: float32 [4, 128], replicated, may hold values from -3 to 3
- prod_cot: bfloat16 [128, 960, 960], P('ch', 'row', 'col'), may hold values from -0.3984375 to 0.3984375
Outputs:
- grad_pair: bfloat16 [960, 960, 128], P(('row', 'ch'), 'col')
- grad_weight: float32 [128, 4, 128], replicated
- grad_bias: float32 [4, 128], replicated
- grad_gain: float32 [128], replicated
- grad_shift: float32 [128], replicated
The draws below stay inside these ranges and needn't reach their ends.
All inputs are finite; a program needn't handle non-finite values.
Results may differ from the reference program's by a relative error of at most 0.015.
Values may be sent and summed in bfloat16 or wider, within the bound.
A program may use at most 192 MiB of HBM per device.

```python
import jax
import jax.numpy as jnp
from jax import lax

CZ = 128
CH = 128
CROP = 960
N_ROW = 8


def draw_pair(key, part):
    key = jax.random.fold_in(key, 7)
    first_key, second_key, third_key = jax.random.split(key, 3)
    entry_scale = jnp.exp(jax.random.uniform(first_key, (CROP, CROP, 1), jnp.float32, 0.0, 2.3))
    channel_scale = jnp.exp(jax.random.uniform(second_key, (1, 1, CZ), jnp.float32, 0.0, 2.3))
    noise_base = jnp.clip(jax.random.normal(third_key, (CROP, CROP, CZ), jnp.float32), -4.0, 4.0)
    return (entry_scale * channel_scale * noise_base).astype(jnp.bfloat16)


def block_levels(stream_key, dims, cuts, low, largest):
    level, own = 1.0, jax.random.fold_in(stream_key, 6)
    for position, shards_of in cuts:
        steps = jnp.exp(jax.random.uniform(jax.random.fold_in(own, position), (shards_of,), jnp.float32, low / len(cuts), largest / len(cuts)))
        level = level * jnp.repeat(steps, dims[position] // shards_of).reshape([-1 if axis == position else 1 for axis in range(len(dims))])
    return level


def scatter_about(stream_key, extent, deviation, reach, cuts=(), dtype=jnp.bfloat16):
    entries = jax.random.normal(stream_key, extent, jnp.float32) * deviation
    if len(cuts) > 0:
        entries = block_levels(stream_key, extent, cuts, -0.22, 0.18) * entries
    return jnp.clip(entries, min=-reach, max=reach).astype(dtype)


def setup_inputs(seed: int = 0) -> dict:
    arg_keys = jax.random.split(jax.random.key(seed), 7)
    pair = draw_pair(jax.random.fold_in(arg_keys[6], 71), 0)
    norm_gain = jnp.clip(1.0 + 0.15 * jax.random.normal(arg_keys[1], (CZ,), jnp.float32), 0.25, 1.75)
    norm_shift = scatter_about(arg_keys[2], (CZ,), 0.5, 3.0, (), jnp.float32)
    proj_weight = scatter_about(arg_keys[3], (CZ, 4, CH), CZ ** -0.5, 0.5)
    proj_bias = scatter_about(arg_keys[4], (4, CH), 0.5, 3.0, (), jnp.float32)
    prod_cot = scatter_about(arg_keys[5], (CH, CROP, CROP), 0.06, 0.3984375, ((0, 4), (1, 8), (2, 4)))
    return dict(pair=pair, norm_gain=norm_gain, norm_shift=norm_shift, proj_weight=proj_weight, proj_bias=proj_bias, prod_cot=prod_cot)


EPSILON = 1e-05

def normalize(pair_rows, norm_gain, norm_shift, proj_weight, proj_bias):
    values = pair_rows.astype(jnp.float32)
    centred = values - lax.optimization_barrier(jnp.mean(values, axis=-1, keepdims=True))
    inv_std = lax.rsqrt(lax.optimization_barrier(jnp.mean(centred * centred, axis=-1, keepdims=True)) + EPSILON)
    scaled = centred * inv_std
    normed = (scaled * norm_gain + norm_shift).astype(jnp.bfloat16)
    linear = jnp.einsum('ikf,fsc->isck', normed.astype(jnp.float32), proj_weight.astype(jnp.float32))
    linear = linear + proj_bias[None, :, :, None]
    return (scaled, inv_std, normed, linear)

def reference(pair, norm_gain, norm_shift, proj_weight, proj_bias, prod_cot):
    block_rows = CROP // N_ROW
    pair_blocks = pair.reshape(N_ROW, block_rows, CROP, CZ)

    def forward_block(pair_rows):
        linear = normalize(pair_rows, norm_gain, norm_shift, proj_weight, proj_bias)[3]
        gate_open = jax.nn.sigmoid(linear[:, 0::2])
        return (gate_open * linear[:, 1::2]).astype(jnp.bfloat16)
    side_values = lax.map(forward_block, pair_blocks).reshape(CROP, 2, CH, CROP)
    left_all = jnp.transpose(side_values[:, 0], (1, 0, 2))
    right_all = jnp.transpose(side_values[:, 1], (1, 0, 2))

    def per_channel(channel_items):
        cotangent, left_one, right_one = channel_items
        left_grad = jnp.dot(cotangent, right_one, preferred_element_type=jnp.float32).astype(jnp.bfloat16)
        cot_blocks = cotangent.reshape(N_ROW, block_rows, CROP).astype(jnp.float32)
        left_blocks = left_one.reshape(N_ROW, block_rows, CROP).astype(jnp.float32)
        block_sums = jnp.einsum('tij,tik->tjk', cot_blocks, left_blocks).astype(jnp.bfloat16)
        block_sums = lax.optimization_barrier(block_sums)
        right_grad = lax.optimization_barrier(jnp.sum(block_sums.astype(jnp.float32), axis=0)).astype(jnp.bfloat16)
        return (left_grad, right_grad)
    left_grads, right_grads = lax.map(per_channel, (prod_cot, left_all, right_all))
    side_grads = jnp.stack([left_grads, right_grads], axis=0)
    side_grads = jnp.transpose(side_grads, (2, 0, 1, 3)).reshape(N_ROW, block_rows, 2, CH, CROP)

    def backward_block(carry, block_items):
        pair_rows, side_grad = block_items
        scaled, inv_std, normed, linear = normalize(pair_rows, norm_gain, norm_shift, proj_weight, proj_bias)
        gate_open = jax.nn.sigmoid(linear[:, 0::2])
        upstream = side_grad.astype(jnp.float32)
        gate_grad = upstream * linear[:, 1::2] * gate_open * (1.0 - gate_open)
        proj_grad = upstream * gate_open
        linear_grad = jnp.stack([gate_grad, proj_grad], axis=2).reshape(block_rows, 4, CH, CROP)
        linear_grad = linear_grad.astype(jnp.bfloat16).astype(jnp.float32)
        normed_grad = jnp.einsum('isck,fsc->ikf', linear_grad, proj_weight.astype(jnp.float32))
        weight_part = jnp.einsum('ikf,isck->fsc', normed.astype(jnp.float32), linear_grad)
        bias_part = lax.optimization_barrier(jnp.sum(linear_grad, axis=(0, 3)))
        gained = normed_grad * norm_gain
        centre_term = lax.optimization_barrier(jnp.mean(gained, axis=-1, keepdims=True))
        slope_term = lax.optimization_barrier(jnp.mean(gained * scaled, axis=-1, keepdims=True))
        pair_grad = ((gained - centre_term - scaled * slope_term) * inv_std).astype(jnp.bfloat16)
        gain_part = lax.optimization_barrier(jnp.sum(normed_grad * scaled, axis=(0, 1)))
        shift_part = lax.optimization_barrier(jnp.sum(normed_grad, axis=(0, 1)))
        new_carry = (carry[0] + weight_part, carry[1] + bias_part, carry[2] + gain_part, carry[3] + shift_part)
        return (new_carry, pair_grad)
    start_carry = (jnp.zeros((CZ, 4, CH), jnp.float32), jnp.zeros((4, CH), jnp.float32), jnp.zeros((CZ,), jnp.float32), jnp.zeros((CZ,), jnp.float32))
    totals, pair_grads = lax.scan(backward_block, start_carry, (pair_blocks, side_grads))
    inverse_crop = 1.0 / CROP
    grad_pair = pair_grads.reshape(CROP, CROP, CZ)
    return (grad_pair, totals[0] * inverse_crop, totals[1] * inverse_crop, totals[2] * inverse_crop, totals[3] * inverse_crop)
```

```python
import functools

import jax
import jax.numpy as jnp
from jax import lax
from jax.experimental import pallas as pl
from jax.experimental.pallas import tpu as pltpu
from jax.sharding import PartitionSpec as P

MESH = pl.DeviceIdType.MESH
EPSILON = 1e-05
CROP = 960
ROWS = 30
COLS = 240
PAIRS = ROWS // 2
HALF_COLS = (128, COLS - 128)
OWNERS = 32
F32, BF16 = jnp.float32, jnp.bfloat16

STEPS = (
    (2, 2),
    (1, 1), (3, 3), (1, 3), (3, 1),
    (1, 2), (2, 1), (3, 2), (2, 3),
    (2, 0), (0, 2),
    (1, 0), (0, 1), (3, 0), (0, 3),
)
OFFSETS = []
for start in range(0, len(STEPS), 1):
    OFFSETS.append((*STEPS[start], 0))
    OFFSETS.append((*STEPS[start], 1))
OFFSETS.append((0, 0, 1))


def kernel(
    pair_ref, cot_ref, wt_ref, wb_ref, bias_ref, gain_ref, shift_ref,
    grad_ref, dw_ref, gs_ref,
    stage, cotf, send1, recv1, left, right, wide, send2, recv2, scaled_s, inv_s, normed_s, acc_gain, acc_shift,
    cs, cr, xs, xr, fs, fr, s1, r1, s2, r2,
):
    row, col, ch = lax.axis_index("row"), lax.axis_index("col"), lax.axis_index("ch")
    me = row * 4 + ch
    z = (ch // 2) * 2 + row // 4
    y = row % 4
    core = ch % 2
    east, west = (col + 1) % 4, (col + 3) % 4

    partners = []
    for dz, dy, dk in OFFSETS:
        z2, y2, k2 = (z + dz) % 4, (y + dy) % 4, (core + dk) % 2
        partners.append(((z2 % 2) * 4 + y2, (z2 // 2) * 2 + k2))

    barrier = pltpu.get_barrier_semaphore()
    for r, g in partners:
        pl.semaphore_signal(barrier, 1, device_id=(r, col, g), device_id_type=MESH)
    for c in (east, west):
        pl.semaphore_signal(barrier, 1, device_id=(row, c, ch), device_id_type=MESH)

    def stage_one(c, carry):
        stage[c] = jnp.zeros((128, 256), BF16)
        stage[c, 0:120, 0:COLS] = cot_ref[c]
        return carry

    lax.fori_loop(0, 32, stage_one, 0)
    pl.semaphore_wait(barrier, len(partners) + 2)

    def cot_copy(c, there):
        return pltpu.make_async_remote_copy(
            src_ref=stage.at[there * 4 + c],
            dst_ref=cotf.at[c, col, pl.ds(row * 128, 128)],
            send_sem=cs.at[c, there], recv_sem=cr.at[c, row],
            device_id=(there, col, ch), device_id_type=MESH,
        )

    def cot_arrival(c, source):
        return pltpu.make_async_remote_copy(
            src_ref=stage.at[c],
            dst_ref=cotf.at[c, col, pl.ds(source * 128, 128)],
            send_sem=cs.at[c, source], recv_sem=cr.at[c, source],
            device_id=(row, col, ch), device_id_type=MESH,
        )

    for c in range(4):
        for step in (6, 5, 7, 2, 4, 1, 3):
            there = ((row // 4 + step // 4) % 2) * 4 + (row + step) % 4
            cot_copy(c, there).start()
        cotf[c, col, pl.ds(row * 128, 128)] = stage[row * 4 + c]

    for c in range(4):
        for b in range(8):
            left[c, b * 128 + 112:(b + 1) * 128] = jnp.zeros((16, 128), BF16)
        for b in range(4):
            right[c, b * 256 + COLS:(b + 1) * 256] = jnp.zeros((16, 128), BF16)
    dw_ref[...] = jnp.zeros_like(dw_ref)
    acc_gain[...] = jnp.zeros_like(acc_gain)
    acc_shift[...] = jnp.zeros_like(acc_shift)

    def forward(kh, ip, carry):
        width = HALF_COLS[kh]
        tokens = []
        for half in range(2):
            x = pair_ref[2 * ip + half, kh * 128:kh * 128 + width].astype(F32)
            if width < 128:
                x = jnp.concatenate([x, jnp.zeros((128 - width, 128), F32)], axis=0)
            tokens.append(x.T)
        x = jnp.concatenate(tokens, axis=1)
        centred = x - jnp.mean(x, axis=0, keepdims=True)
        inv_std = lax.rsqrt(jnp.mean(centred * centred, axis=0, keepdims=True) + EPSILON)
        scaled = centred * inv_std
        normed = (scaled * gain_ref[...] + shift_ref[...]).astype(BF16)
        slot = kh * PAIRS + ip
        scaled_s[slot] = scaled
        inv_s[slot] = inv_std
        normed_s[slot, 0:128] = normed
        normed_s[slot, 128:144] = jnp.ones((16, 256), BF16)
        linear = jnp.dot(wt_ref[...], normed, preferred_element_type=F32) + bias_ref[...]
        gate = 0.5 * jnp.tanh(0.5 * linear[0:256]) + 0.5
        side = gate * linear[256:512]
        if width < 128:
            lane = lax.broadcasted_iota(jnp.int32, (256, 256), 1)
            side = jnp.where(lane % 128 < width, side, 0.0)
        packed = jnp.concatenate(
            [side[:, 0:128].reshape(OWNERS, 8, 128), side[:, 128:256].reshape(OWNERS, 8, 128)], axis=1
        ).astype(BF16)
        send1[kh, :, pl.ds(pl.multiple_of(ip * 16, 16), 16), :] = packed
        return carry

    def exchange(source, target, send_sem, recv_sem, kh, there_r, there_g):
        there = there_r * 4 + there_g
        return pltpu.make_async_remote_copy(
            src_ref=source.at[kh, there], dst_ref=target.at[kh, me],
            send_sem=send_sem.at[kh, there], recv_sem=recv_sem.at[kh, me],
            device_id=(there_r, col, there_g), device_id_type=MESH,
        )

    def arrival(source, target, send_sem, recv_sem, kh, there):
        return pltpu.make_async_remote_copy(
            src_ref=source.at[kh, there], dst_ref=target.at[kh, there],
            send_sem=send_sem.at[kh, there], recv_sem=recv_sem.at[kh, there],
            device_id=(row, col, ch), device_id_type=MESH,
        )

    def send_all(source, target, send_sem, recv_sem, kh):
        for r, g in partners:
            exchange(source, target, send_sem, recv_sem, kh, r, g).start()
        target[kh, me] = source[kh, me]

    def others(action):
        def one(there, carry):
            @pl.when(there != me)
            def _():
                action(there)
            return carry

        lax.fori_loop(0, OWNERS, one, 0)

    def x_copy(c, block, part, sems, recvs, side, there):
        return pltpu.make_async_remote_copy(
            src_ref=cotf.at[c, block, part], dst_ref=cotf.at[c, block, part],
            send_sem=sems.at[c, side], recv_sem=recvs.at[c, side],
            device_id=(row, there, ch), device_id_type=MESH,
        )

    WHOLE, LOW, HIGH = pl.ds(0, 1024), pl.ds(0, 512), pl.ds(512, 512)
    far = (col + 2) % 4

    def x_send(c):
        def one(source, carry):
            @pl.when(source != row)
            def _():
                cot_arrival(c, source).wait_recv()
            return carry

        lax.fori_loop(0, 8, one, 0)
        x_copy(c, col, WHOLE, xs, xr, 0, east).start()
        x_copy(c, col, WHOLE, xs, xr, 1, west).start()

    def x_forward(c):
        x_copy(c, west, WHOLE, xs, xr, 0, east).wait_recv()
        x_copy(c, west, LOW, fs, fr, 0, east).start()
        x_copy(c, east, WHOLE, xs, xr, 1, west).wait_recv()
        x_copy(c, east, HIGH, fs, fr, 1, west).start()

    def x_finish(c):
        x_copy(c, far, LOW, fs, fr, 0, east).wait_recv()
        x_copy(c, far, HIGH, fs, fr, 1, west).wait_recv()

    def regroup(kh):
        others(lambda there: arrival(send1, recv1, s1, r1, kh, there).wait_recv())

        def widen(source, carry):
            wide[pl.ds(pl.multiple_of(source * 240, 8), 240)] = recv1[kh, source].astype(F32)
            return carry

        lax.fori_loop(0, OWNERS, widen, 0)
        for c in range(4):
            for b in range(8):
                left[c, b * 128:b * 128 + 120] = wide[pl.ds(b * 960 + c, 120, stride=8)].astype(BF16)
            for b in range(4):
                right[c, b * 256:b * 256 + COLS] = wide[pl.ds(b * 1920 + 4 + c, COLS, stride=8)].astype(BF16)

    def triangle(c):
        for b in range(8):
            rows = pl.ds(b * 128, 128)
            total = jnp.zeros((128, 128), F32)
            for x in range(4):
                total += jnp.dot(cotf[c, x, rows], right[c, x * 256:(x + 1) * 256], preferred_element_type=F32)
            wide[pl.ds(b * 960 + c, 120, stride=8)] = total[0:120]
        for x in range(4):
            total = lax.dot_general(
                cotf[c, x], left[c], (((0,), (0,)), ((), ())), preferred_element_type=F32
            )
            wide[pl.ds(x * 1920 + 4 + c, COLS, stride=8)] = total[0:COLS]

    def give_back(kh):
        def narrow(target, carry):
            send2[kh, target] = wide[pl.ds(pl.multiple_of(target * 240, 8), 240)].astype(BF16)
            return carry

        lax.fori_loop(0, OWNERS, narrow, 0)
        send_all(send2, recv2, s2, r2, kh)

    def backward(kh, ip, carry):
        width = HALF_COLS[kh]
        slot = kh * PAIRS + ip
        back = recv2[kh, :, pl.ds(pl.multiple_of(ip * 16, 16), 16), :].astype(F32)
        side_grad = jnp.concatenate(
            [back[:, 0:8].reshape(256, 128), back[:, 8:16].reshape(256, 128)], axis=1
        )
        normed = normed_s[slot, 0:128]
        linear = jnp.dot(wt_ref[...], normed, preferred_element_type=F32) + bias_ref[...]
        gate = 0.5 * jnp.tanh(0.5 * linear[0:256]) + 0.5
        value_grad = side_grad * gate
        gate_grad = value_grad * linear[256:512] * (1.0 - gate)
        linear_grad = jnp.concatenate([gate_grad.astype(BF16), value_grad.astype(BF16)], axis=0)
        normed_grad = jnp.dot(wb_ref[...], linear_grad, preferred_element_type=F32)
        dw_ref[...] += lax.dot_general(
            linear_grad, normed_s[slot], (((1,), (1,)), ((), ())), preferred_element_type=F32
        )
        scaled = scaled_s[slot]
        acc_gain[...] += normed_grad * scaled
        acc_shift[...] += normed_grad
        gained = normed_grad * gain_ref[...]
        centre = jnp.mean(gained, axis=0, keepdims=True)
        slope = jnp.mean(gained * scaled, axis=0, keepdims=True)
        result = (gained - centre - scaled * slope) * inv_s[slot]
        for half in range(2):
            out = result[:, half * 128:(half + 1) * 128].T.astype(BF16)
            grad_ref[2 * ip + half, kh * 128:kh * 128 + width] = out[0:width]
        return carry

    lax.fori_loop(0, PAIRS, functools.partial(forward, 0), 0)
    send_all(send1, recv1, s1, r1, 0)
    x_send(0)
    lax.fori_loop(0, 8, functools.partial(forward, 1), 0)
    x_send(1)
    lax.fori_loop(8, PAIRS, functools.partial(forward, 1), 0)
    send_all(send1, recv1, s1, r1, 1)
    x_send(2)
    x_forward(0)
    x_send(3)
    x_forward(1)
    regroup(0)
    x_forward(2)
    x_finish(0)
    triangle(0)
    x_forward(3)
    for c in range(1, 4):
        x_finish(c)
        triangle(c)
    give_back(0)
    regroup(1)
    for c in range(4):
        triangle(c)
    give_back(1)
    for kh in range(2):
        others(lambda there: arrival(send2, recv2, s2, r2, kh, there).wait_recv())
        lax.fori_loop(0, PAIRS, functools.partial(backward, kh), 0)
    gs_ref[0] = jnp.sum(acc_gain[...].T, axis=0, keepdims=True)
    gs_ref[1] = jnp.sum(acc_shift[...].T, axis=0, keepdims=True)

    for c in range(4):
        def sent(there, carry):
            @pl.when(there != row)
            def _():
                cot_copy(c, there).wait_send()
            return carry

        lax.fori_loop(0, 8, sent, 0)
        x_copy(c, col, WHOLE, xs, xr, 0, east).wait_send()
        x_copy(c, col, WHOLE, xs, xr, 1, west).wait_send()
        x_copy(c, west, LOW, fs, fr, 0, east).wait_send()
        x_copy(c, east, HIGH, fs, fr, 1, west).wait_send()
    for kh in range(2):
        others(lambda there: arrival(send1, recv1, s1, r1, kh, there).wait_send())
        others(lambda there: arrival(send2, recv2, s2, r2, kh, there).wait_send())


def by_owner(array):
    lead = array.shape[:-2]
    n = len(lead)
    parts = array.reshape(*lead, 2, 2, 4, 8, 4)
    axes = tuple(range(n)) + tuple(n + a for a in (1, 3, 2, 0, 4))
    return parts.transpose(axes).reshape(*lead, 512)


def by_stream(array):
    lead = array.shape[:-1]
    n = len(lead)
    parts = array.reshape(*lead, 2, 8, 4, 2, 4)
    axes = tuple(range(n)) + tuple(n + a for a in (3, 0, 2, 1, 4))
    return parts.transpose(axes).reshape(*lead, 4, 128)


def shards(pair, norm_gain, norm_shift, proj_weight, proj_bias, prod_cot):
    wb = by_owner(proj_weight)
    wt = wb.T
    bias = jnp.broadcast_to(by_owner(proj_bias)[:, None], (512, 256))
    gain = jnp.broadcast_to(norm_gain[:, None], (128, 256))
    shift = jnp.broadcast_to(norm_shift[:, None], (128, 256))
    vmem = pl.BlockSpec(memory_space=pltpu.VMEM)
    dma = pltpu.SemaphoreType.DMA
    grad_pair, dw, gs = pl.pallas_call(
        kernel,
        out_shape=(
            jax.ShapeDtypeStruct((ROWS, COLS, 128), BF16),
            jax.ShapeDtypeStruct((512, 144), F32),
            jax.ShapeDtypeStruct((2, 1, 128), F32),
        ),
        in_specs=[vmem] * 7,
        out_specs=(vmem,) * 3,
        scratch_shapes=[
            pltpu.VMEM((32, 128, 256), BF16),
            pltpu.VMEM((4, 4, 1024, 256), BF16),
            pltpu.VMEM((2, OWNERS, 240, 128), BF16),
            pltpu.VMEM((2, OWNERS, 240, 128), BF16),
            pltpu.VMEM((4, 1024, 128), BF16),
            pltpu.VMEM((4, 1024, 128), BF16),
            pltpu.VMEM((CROP * 8, 128), F32),
            pltpu.VMEM((2, OWNERS, 240, 128), BF16),
            pltpu.VMEM((2, OWNERS, 240, 128), BF16),
            pltpu.VMEM((2 * PAIRS, 128, 256), F32),
            pltpu.VMEM((2 * PAIRS, 1, 256), F32),
            pltpu.VMEM((2 * PAIRS, 144, 256), BF16),
            pltpu.VMEM((128, 256), F32),
            pltpu.VMEM((128, 256), F32),
            dma((4, 8)), dma((4, 8)), dma((4, 2)), dma((4, 2)), dma((4, 2)), dma((4, 2)),
            dma((2, OWNERS)), dma((2, OWNERS)), dma((2, OWNERS)), dma((2, OWNERS)),
        ],
        compiler_params=pltpu.CompilerParams(
            collective_id=0, has_side_effects=True, vmem_limit_bytes=60 << 20
        ),
        name="triangle_backward",
    )(pair, prod_cot, wt, wb, bias, gain, shift)
    sums = jnp.concatenate(
        [dw[:, 0:128], dw[:, 128].reshape(4, 128), gs.reshape(2, 128)], axis=0
    )
    sums = lax.psum(sums, ("row", "col", "ch")) * (1.0 / CROP)
    grad_weight = by_stream(sums[0:512].T)
    grad_bias = by_stream(sums[512:516].reshape(512))
    return grad_pair, grad_weight, grad_bias, sums[516], sums[517]


def solution(mesh):
    in_specs = (P(("row", "ch"), "col", None), P(), P(), P(), P(), P("ch", "row", "col"))
    out_specs = (P(("row", "ch"), "col", None), P(), P(), P(), P())
    return jax.shard_map(shards, mesh=mesh, in_specs=in_specs, out_specs=out_specs, check_vma=False)
```

```python
import functools

import jax
import jax.numpy as jnp
from jax import lax
from jax.experimental import pallas as pl
from jax.experimental.pallas import tpu as pltpu
from jax.sharding import PartitionSpec as P

MESH = pl.DeviceIdType.MESH
EPSILON = 1e-05
CROP = 960
ROWS = 30
COLS = 240
PAIRS = ROWS // 2
HALF_COLS = (128, COLS - 128)
OWNERS = 32
F32, BF16 = jnp.float32, jnp.bfloat16

STEPS = (
    (2, 2),
    (1, 1), (3, 3), (1, 3), (3, 1),
    (1, 2), (2, 1), (3, 2), (2, 3),
    (2, 0), (0, 2),
    (1, 0), (0, 1), (3, 0), (0, 3),
)
OFFSETS = []
for start in range(0, len(STEPS), 1):
    OFFSETS.append((*STEPS[start], 0))
    OFFSETS.append((*STEPS[start], 1))
OFFSETS.append((0, 0, 1))


GROUPS = [(kind, t, side) for kind in range(2) for t in range(OWNERS) for side in range(2)]


def owner_row(kind, t, side):
    return kind * 256 + t * 8 + side * 4


def stream_row(kind, t, side):
    return (side * 2 + kind) * 128 + (t % 4) * 32 + (t // 4) * 4


def kernel(
    pair_ref, cot_ref, weight_ref, biases_ref, norm_ref,
    grad_ref, dw_ref, small_ref,
    stage, cotf, send1, recv1, left, right, wide, send2, recv2, scaled_s, inv_s, normed_s, acc_gain, acc_shift,
    wt_ref, wb_ref, bias_ref, gain_ref, shift_ref, natural, owned, acc, small, part_s, part_r, line, whole,
    cs, cr, xs, xr, fs, fr, s1, r1, s2, r2, as_, ar, bs, br, gs_, gr,
):
    row, col, ch = lax.axis_index("row"), lax.axis_index("col"), lax.axis_index("ch")
    me = row * 4 + ch
    z = (ch // 2) * 2 + row // 4
    y = row % 4
    core = ch % 2
    east, west, far = (col + 1) % 4, (col + 3) % 4, (col + 2) % 4

    partners = []
    for dz, dy, dk in OFFSETS:
        z2, y2, k2 = (z + dz) % 4, (y + dy) % 4, (core + dk) % 2
        partners.append(((z2 % 2) * 4 + y2, (z2 // 2) * 2 + k2))

    barrier = pltpu.get_barrier_semaphore()
    for r, g in partners:
        pl.semaphore_signal(barrier, 1, device_id=(r, col, g), device_id_type=MESH)
    for c in (east, west, far):
        pl.semaphore_signal(barrier, 1, device_id=(row, c, ch), device_id_type=MESH)

    def stage_one(c, carry):
        stage[c] = jnp.zeros((128, 256), BF16)
        stage[c, 0:120, 0:COLS] = cot_ref[c]
        return carry

    lax.fori_loop(0, 32, stage_one, 0)
    pl.semaphore_wait(barrier, len(partners) + 3)

    def cot_copy(c, there):
        return pltpu.make_async_remote_copy(
            src_ref=stage.at[there * 4 + c],
            dst_ref=cotf.at[c, col, pl.ds(row * 128, 128)],
            send_sem=cs.at[c, there], recv_sem=cr.at[c, row],
            device_id=(there, col, ch), device_id_type=MESH,
        )

    def cot_arrival(c, source):
        return pltpu.make_async_remote_copy(
            src_ref=stage.at[c],
            dst_ref=cotf.at[c, col, pl.ds(source * 128, 128)],
            send_sem=cs.at[c, source], recv_sem=cr.at[c, source],
            device_id=(row, col, ch), device_id_type=MESH,
        )

    for c in range(4):
        for step in (6, 5, 7, 2, 4, 1, 3):
            there = ((row // 4 + step // 4) % 2) * 4 + (row + step) % 4
            cot_copy(c, there).start()
        cotf[c, col, pl.ds(row * 128, 128)] = stage[row * 4 + c]

    def to_owners():
        for kind, t, side in GROUPS:
            owned[owner_row(kind, t, side):owner_row(kind, t, side) + 4] = natural[
                stream_row(kind, t, side):stream_row(kind, t, side) + 4
            ]

    def to_streams():
        for kind, t, side in GROUPS:
            natural[stream_row(kind, t, side):stream_row(kind, t, side) + 4] = owned[
                owner_row(kind, t, side):owner_row(kind, t, side) + 4
            ]

    for s in range(4):
        natural[s * 128:(s + 1) * 128] = weight_ref[:, s * 128:(s + 1) * 128].astype(F32).T
    to_owners()
    wt_ref[...] = owned[...].astype(BF16)
    for s in range(4):
        wb_ref[:, s * 128:(s + 1) * 128] = owned[s * 128:(s + 1) * 128].T.astype(BF16)
    for s in range(4):
        natural[s * 128:(s + 1) * 128] = jnp.broadcast_to(biases_ref[s:s + 1], (128, 128)).T
    to_owners()
    for half in range(2):
        lanes = slice(half * 128, (half + 1) * 128)
        bias_ref[:, lanes] = owned[...]
        gain_ref[:, lanes] = jnp.broadcast_to(norm_ref[0:1], (128, 128)).T
        shift_ref[:, lanes] = jnp.broadcast_to(norm_ref[1:2], (128, 128)).T

    for c in range(4):
        for b in range(8):
            left[c, b * 128 + 112:(b + 1) * 128] = jnp.zeros((16, 128), BF16)
        for b in range(4):
            right[c, b * 256 + COLS:(b + 1) * 256] = jnp.zeros((16, 128), BF16)
    acc[...] = jnp.zeros_like(acc)
    small[...] = jnp.zeros_like(small)
    acc_gain[...] = jnp.zeros_like(acc_gain)
    acc_shift[...] = jnp.zeros_like(acc_shift)

    def forward(kh, ip, carry):
        width = HALF_COLS[kh]
        tokens = []
        for half in range(2):
            x = pair_ref[2 * ip + half, kh * 128:kh * 128 + width].astype(F32)
            if width < 128:
                x = jnp.concatenate([x, jnp.zeros((128 - width, 128), F32)], axis=0)
            tokens.append(x.T)
        x = jnp.concatenate(tokens, axis=1)
        centred = x - jnp.mean(x, axis=0, keepdims=True)
        inv_std = lax.rsqrt(jnp.mean(centred * centred, axis=0, keepdims=True) + EPSILON)
        scaled = centred * inv_std
        normed = (scaled * gain_ref[...] + shift_ref[...]).astype(BF16)
        slot = kh * PAIRS + ip
        scaled_s[slot] = scaled
        inv_s[slot] = inv_std
        normed_s[slot, 0:128] = normed
        normed_s[slot, 128:144] = jnp.ones((16, 256), BF16)
        linear = jnp.dot(wt_ref[...], normed, preferred_element_type=F32) + bias_ref[...]
        gate = 0.5 * jnp.tanh(0.5 * linear[0:256]) + 0.5
        side = gate * linear[256:512]
        if width < 128:
            lane = lax.broadcasted_iota(jnp.int32, (256, 256), 1)
            side = jnp.where(lane % 128 < width, side, 0.0)
        packed = jnp.concatenate(
            [side[:, 0:128].reshape(OWNERS, 8, 128), side[:, 128:256].reshape(OWNERS, 8, 128)], axis=1
        ).astype(BF16)
        send1[kh, :, pl.ds(pl.multiple_of(ip * 16, 16), 16), :] = packed
        return carry

    def exchange(source, target, send_sem, recv_sem, kh, there_r, there_g):
        there = there_r * 4 + there_g
        return pltpu.make_async_remote_copy(
            src_ref=source.at[kh, there], dst_ref=target.at[kh, me],
            send_sem=send_sem.at[kh, there], recv_sem=recv_sem.at[kh, me],
            device_id=(there_r, col, there_g), device_id_type=MESH,
        )

    def arrival(source, target, send_sem, recv_sem, kh, there):
        return pltpu.make_async_remote_copy(
            src_ref=source.at[kh, there], dst_ref=target.at[kh, there],
            send_sem=send_sem.at[kh, there], recv_sem=recv_sem.at[kh, there],
            device_id=(row, col, ch), device_id_type=MESH,
        )

    def send_all(source, target, send_sem, recv_sem, kh):
        for r, g in partners:
            exchange(source, target, send_sem, recv_sem, kh, r, g).start()
        target[kh, me] = source[kh, me]

    def others(action):
        def one(there, carry):
            @pl.when(there != me)
            def _():
                action(there)
            return carry

        lax.fori_loop(0, OWNERS, one, 0)

    def x_copy(c, block, part, sems, recvs, side, there):
        return pltpu.make_async_remote_copy(
            src_ref=cotf.at[c, block, part], dst_ref=cotf.at[c, block, part],
            send_sem=sems.at[c, side], recv_sem=recvs.at[c, side],
            device_id=(row, there, ch), device_id_type=MESH,
        )

    WHOLE, LOW, HIGH = pl.ds(0, 1024), pl.ds(0, 512), pl.ds(512, 512)

    def x_send(c):
        def one(source, carry):
            @pl.when(source != row)
            def _():
                cot_arrival(c, source).wait_recv()
            return carry

        lax.fori_loop(0, 8, one, 0)
        x_copy(c, col, WHOLE, xs, xr, 0, east).start()
        x_copy(c, col, WHOLE, xs, xr, 1, west).start()

    def x_forward(c):
        x_copy(c, west, WHOLE, xs, xr, 0, east).wait_recv()
        x_copy(c, west, LOW, fs, fr, 0, east).start()
        x_copy(c, east, WHOLE, xs, xr, 1, west).wait_recv()
        x_copy(c, east, HIGH, fs, fr, 1, west).start()

    def x_finish(c):
        x_copy(c, far, LOW, fs, fr, 0, east).wait_recv()
        x_copy(c, far, HIGH, fs, fr, 1, west).wait_recv()

    def regroup(kh):
        others(lambda there: arrival(send1, recv1, s1, r1, kh, there).wait_recv())

        def widen(source, carry):
            wide[pl.ds(pl.multiple_of(source * 240, 8), 240)] = recv1[kh, source].astype(F32)
            return carry

        lax.fori_loop(0, OWNERS, widen, 0)
        for c in range(4):
            for b in range(8):
                left[c, b * 128:b * 128 + 120] = wide[pl.ds(b * 960 + c, 120, stride=8)].astype(BF16)
            for b in range(4):
                right[c, b * 256:b * 256 + COLS] = wide[pl.ds(b * 1920 + 4 + c, COLS, stride=8)].astype(BF16)

    def triangle(c):
        for b in range(8):
            rows = pl.ds(b * 128, 128)
            total = jnp.zeros((128, 128), F32)
            for x in range(4):
                total += jnp.dot(cotf[c, x, rows], right[c, x * 256:(x + 1) * 256], preferred_element_type=F32)
            wide[pl.ds(b * 960 + c, 120, stride=8)] = total[0:120]
        for x in range(4):
            total = lax.dot_general(
                cotf[c, x], left[c], (((0,), (0,)), ((), ())), preferred_element_type=F32
            )
            wide[pl.ds(x * 1920 + 4 + c, COLS, stride=8)] = total[0:COLS]

    def give_back(kh):
        def narrow(target, carry):
            send2[kh, target] = wide[pl.ds(pl.multiple_of(target * 240, 8), 240)].astype(BF16)
            return carry

        lax.fori_loop(0, OWNERS, narrow, 0)
        send_all(send2, recv2, s2, r2, kh)

    def backward(kh, ip, carry):
        width = HALF_COLS[kh]
        slot = kh * PAIRS + ip
        back = recv2[kh, :, pl.ds(pl.multiple_of(ip * 16, 16), 16), :].astype(F32)
        side_grad = jnp.concatenate(
            [back[:, 0:8].reshape(256, 128), back[:, 8:16].reshape(256, 128)], axis=1
        )
        normed = normed_s[slot, 0:128]
        linear = jnp.dot(wt_ref[...], normed, preferred_element_type=F32) + bias_ref[...]
        gate = 0.5 * jnp.tanh(0.5 * linear[0:256]) + 0.5
        value_grad = side_grad * gate
        gate_grad = value_grad * linear[256:512] * (1.0 - gate)
        linear_grad = jnp.concatenate([gate_grad.astype(BF16), value_grad.astype(BF16)], axis=0)
        normed_grad = jnp.dot(wb_ref[...], linear_grad, preferred_element_type=F32)
        acc[...] += lax.dot_general(
            normed_s[slot], linear_grad, (((1,), (1,)), ((), ())), preferred_element_type=F32
        )
        scaled = scaled_s[slot]
        acc_gain[...] += normed_grad * scaled
        acc_shift[...] += normed_grad
        gained = normed_grad * gain_ref[...]
        centre = jnp.mean(gained, axis=0, keepdims=True)
        slope = jnp.mean(gained * scaled, axis=0, keepdims=True)
        result = (gained - centre - scaled * slope) * inv_s[slot]
        for half in range(2):
            out = result[:, half * 128:(half + 1) * 128].T.astype(BF16)
            grad_ref[2 * ip + half, kh * 128:kh * 128 + width] = out[0:width]
        return carry

    lax.fori_loop(0, PAIRS, functools.partial(forward, 0), 0)
    send_all(send1, recv1, s1, r1, 0)
    x_send(0)
    lax.fori_loop(0, 8, functools.partial(forward, 1), 0)
    x_send(1)
    lax.fori_loop(8, PAIRS, functools.partial(forward, 1), 0)
    send_all(send1, recv1, s1, r1, 1)
    x_send(2)
    x_forward(0)
    x_send(3)
    x_forward(1)
    regroup(0)
    x_forward(2)
    x_finish(0)
    triangle(0)
    x_forward(3)
    for c in range(1, 4):
        x_finish(c)
        triangle(c)
    give_back(0)
    regroup(1)
    for c in range(4):
        triangle(c)
    give_back(1)
    for kh in range(2):
        others(lambda there: arrival(send2, recv2, s2, r2, kh, there).wait_recv())
        lax.fori_loop(0, PAIRS, functools.partial(backward, kh), 0)

    for s in range(4):
        small[s:s + 1] = acc[128:129, s * 128:(s + 1) * 128]
    small[4:5] = jnp.sum(acc_gain[...].T, axis=0, keepdims=True)
    small[5:6] = jnp.sum(acc_shift[...].T, axis=0, keepdims=True)
    for o in range(OWNERS):
        rows, lane = slice((o // 2) * 8, (o // 2) * 8 + 8), (o % 2) * 256
        part_s[o, 0:8] = acc[rows, lane:lane + 128]
        part_s[o, 8:16] = acc[rows, lane + 128:lane + 256]
        part_s[o, 16:24] = small[...]
    for r, g in partners:
        there = r * 4 + g
        pltpu.make_async_remote_copy(
            src_ref=part_s.at[there], dst_ref=part_r.at[me], send_sem=as_.at[there], recv_sem=ar.at[me],
            device_id=(r, col, g), device_id_type=MESH,
        ).start()
    part_r[me] = part_s[me]

    def part_arrival(there):
        return pltpu.make_async_remote_copy(
            src_ref=part_s.at[there], dst_ref=part_r.at[there], send_sem=as_.at[there], recv_sem=ar.at[there],
            device_id=(row, col, ch), device_id_type=MESH,
        )

    others(lambda there: part_arrival(there).wait_recv())
    total = part_r[0]
    for o in range(1, OWNERS):
        total = total + part_r[o]
    line[col] = total

    def line_copy(slot, there):
        return pltpu.make_async_remote_copy(
            src_ref=line.at[slot], dst_ref=line.at[slot], send_sem=bs.at[there], recv_sem=br.at[slot],
            device_id=(row, there, ch), device_id_type=MESH,
        )

    for there in (far, east, west):
        line_copy(col, there).start()
    for there in (far, east, west):
        line_copy(there, there).wait_recv()
    total = (line[0] + line[1]) + (line[2] + line[3])
    total = total * (1.0 / CROP)
    whole[me] = total[0:16]
    small_ref[...] = total[16:24]

    def whole_copy(slot, there, r, g):
        return pltpu.make_async_remote_copy(
            src_ref=whole.at[slot], dst_ref=whole.at[slot], send_sem=gs_.at[there], recv_sem=gr.at[slot],
            device_id=(r, col, g), device_id_type=MESH,
        )

    for r, g in partners:
        whole_copy(me, r * 4 + g, r, g).start()
    others(lambda there: whole_copy(there, there, row, ch).wait_recv())
    for o in range(OWNERS):
        rows, lane = slice((o // 2) * 8, (o // 2) * 8 + 8), (o % 2) * 256
        acc[rows, lane:lane + 128] = whole[o, 0:8]
        acc[rows, lane + 128:lane + 256] = whole[o, 8:16]
    for s in range(4):
        owned[s * 128:(s + 1) * 128] = acc[0:128, s * 128:(s + 1) * 128].T
    to_streams()
    for s in range(4):
        dw_ref[:, s * 128:(s + 1) * 128] = natural[s * 128:(s + 1) * 128].T
    for s in range(4):
        owned[s * 128:(s + 1) * 128] = jnp.broadcast_to(small_ref[s:s + 1], (128, 128)).T
    to_streams()
    for s in range(4):
        small_ref[s:s + 1] = natural[s * 128:(s + 1) * 128].T[0:1]

    others(lambda there: part_arrival(there).wait_send())
    others(lambda there: whole_copy(me, there, row, ch).wait_send())
    for there in (far, east, west):
        line_copy(col, there).wait_send()
    for c in range(4):
        def sent(there, carry):
            @pl.when(there != row)
            def _():
                cot_copy(c, there).wait_send()
            return carry

        lax.fori_loop(0, 8, sent, 0)
        x_copy(c, col, WHOLE, xs, xr, 0, east).wait_send()
        x_copy(c, col, WHOLE, xs, xr, 1, west).wait_send()
        x_copy(c, west, LOW, fs, fr, 0, east).wait_send()
        x_copy(c, east, HIGH, fs, fr, 1, west).wait_send()
    for kh in range(2):
        others(lambda there: arrival(send1, recv1, s1, r1, kh, there).wait_send())
        others(lambda there: arrival(send2, recv2, s2, r2, kh, there).wait_send())


def shards(pair, norm_gain, norm_shift, proj_weight, proj_bias, prod_cot):
    vmem = pl.BlockSpec(memory_space=pltpu.VMEM)
    dma = pltpu.SemaphoreType.DMA
    grad_pair, dw, small = pl.pallas_call(
        kernel,
        out_shape=(
            jax.ShapeDtypeStruct((ROWS, COLS, 128), BF16),
            jax.ShapeDtypeStruct((128, 512), F32),
            jax.ShapeDtypeStruct((8, 128), F32),
        ),
        in_specs=[vmem] * 5,
        out_specs=(vmem,) * 3,
        scratch_shapes=[
            pltpu.VMEM((32, 128, 256), BF16),
            pltpu.VMEM((4, 4, 1024, 256), BF16),
            pltpu.VMEM((2, OWNERS, 240, 128), BF16),
            pltpu.VMEM((2, OWNERS, 240, 128), BF16),
            pltpu.VMEM((4, 1024, 128), BF16),
            pltpu.VMEM((4, 1024, 128), BF16),
            pltpu.VMEM((CROP * 8, 128), F32),
            pltpu.VMEM((2, OWNERS, 240, 128), BF16),
            pltpu.VMEM((2, OWNERS, 240, 128), BF16),
            pltpu.VMEM((2 * PAIRS, 128, 256), F32),
            pltpu.VMEM((2 * PAIRS, 1, 256), F32),
            pltpu.VMEM((2 * PAIRS, 144, 256), BF16),
            pltpu.VMEM((128, 256), F32),
            pltpu.VMEM((128, 256), F32),
            pltpu.VMEM((512, 128), BF16),
            pltpu.VMEM((128, 512), BF16),
            pltpu.VMEM((512, 256), F32),
            pltpu.VMEM((128, 256), F32),
            pltpu.VMEM((128, 256), F32),
            pltpu.VMEM((512, 128), F32),
            pltpu.VMEM((512, 128), F32),
            pltpu.VMEM((144, 512), F32),
            pltpu.VMEM((8, 128), F32),
            pltpu.VMEM((OWNERS, 24, 128), F32),
            pltpu.VMEM((OWNERS, 24, 128), F32),
            pltpu.VMEM((4, 24, 128), F32),
            pltpu.VMEM((OWNERS, 16, 128), F32),
            dma((4, 8)), dma((4, 8)), dma((4, 2)), dma((4, 2)), dma((4, 2)), dma((4, 2)),
            dma((2, OWNERS)), dma((2, OWNERS)), dma((2, OWNERS)), dma((2, OWNERS)),
            dma((OWNERS,)), dma((OWNERS,)), dma((4,)), dma((4,)), dma((OWNERS,)), dma((OWNERS,)),
        ],
        compiler_params=pltpu.CompilerParams(
            collective_id=0, has_side_effects=True, vmem_limit_bytes=60 << 20
        ),
        name="triangle_backward",
    )(pair, prod_cot, proj_weight.reshape(128, 512), proj_bias, jnp.stack([norm_gain, norm_shift]))
    return grad_pair, dw.reshape(128, 4, 128), small[0:4], small[4], small[5]


def solution(mesh):
    in_specs = (P(("row", "ch"), "col", None), P(), P(), P(), P(), P("ch", "row", "col"))
    out_specs = (P(("row", "ch"), "col", None), P(), P(), P(), P())
    return jax.shard_map(shards, mesh=mesh, in_specs=in_specs, out_specs=out_specs, check_vma=False)
```

```python
import functools

import jax
import jax.numpy as jnp
from jax import lax
from jax.experimental import pallas as pl
from jax.experimental.pallas import tpu as pltpu
from jax.sharding import PartitionSpec as P

MESH = pl.DeviceIdType.MESH
EPSILON = 1e-05
CROP = 960
ROWS = 30
COLS = 240
PAIRS = ROWS // 2
HALF_COLS = (128, COLS - 128)
OWNERS = 32
F32, BF16 = jnp.float32, jnp.bfloat16

STEPS = (
    (2, 2),
    (1, 1), (3, 3), (1, 3), (3, 1),
    (1, 2), (2, 1), (3, 2), (2, 3),
    (2, 0), (0, 2),
    (1, 0), (0, 1), (3, 0), (0, 3),
)
OFFSETS = []
for start in range(0, len(STEPS), 1):
    OFFSETS.append((*STEPS[start], 0))
    OFFSETS.append((*STEPS[start], 1))
OFFSETS.append((0, 0, 1))


BACK_CHUNKS = ((0, 0, PAIRS), (1, 0, 8), (1, 8, PAIRS))
BACK = ((0,), (1, 2))
GROUPS = [(kind, t, side) for kind in range(2) for t in range(OWNERS) for side in range(2)]


def owner_row(kind, t, side):
    return kind * 256 + t * 8 + side * 4


def stream_row(kind, t, side):
    return (side * 2 + kind) * 128 + (t % 4) * 32 + (t // 4) * 4


def kernel(
    pair_ref, cot_ref, weight_ref, biases_ref, gains_ref, shifts_ref,
    grad_ref, dw_ref, small_ref,
    stage, cotf, send1, recv1, left, right, wide, send2, recv2, scaled_s, inv_s, normed_s, acc_gain, acc_shift,
    wt_ref, wb_ref, bias_ref, gain_ref, shift_ref, natural, owned, acc, small, part_s, part_r, line, whole,
    cs, cr, xs, xr, fs, fr, s1, r1, s2, r2, as_, ar, bs, br, gs_, gr,
):
    row, col, ch = lax.axis_index("row"), lax.axis_index("col"), lax.axis_index("ch")
    me = row * 4 + ch
    z = (ch // 2) * 2 + row // 4
    y = row % 4
    core = ch % 2
    east, west, far = (col + 1) % 4, (col + 3) % 4, (col + 2) % 4

    partners = []
    for dz, dy, dk in OFFSETS:
        z2, y2, k2 = (z + dz) % 4, (y + dy) % 4, (core + dk) % 2
        partners.append(((z2 % 2) * 4 + y2, (z2 // 2) * 2 + k2))

    barrier = pltpu.get_barrier_semaphore()
    for r, g in partners:
        pl.semaphore_signal(barrier, 1, device_id=(r, col, g), device_id_type=MESH)
    for c in (east, west, far):
        pl.semaphore_signal(barrier, 1, device_id=(row, c, ch), device_id_type=MESH)

    def stage_one(pair, carry):
        stage[pair] = jnp.zeros((240, 256), BF16)
        stage[pair, 0:120, 0:COLS] = cot_ref[2 * pair]
        stage[pair, 120:240, 0:COLS] = cot_ref[2 * pair + 1]
        return carry

    lax.fori_loop(0, 16, stage_one, 0)
    pl.semaphore_wait(barrier, len(partners) + 3)

    def cot_copy(there):
        return pltpu.make_async_remote_copy(
            src_ref=stage.at[pl.ds(there * 2, 2)], dst_ref=cotf.at[col, row],
            send_sem=cs.at[there], recv_sem=cr.at[row],
            device_id=(there, col, ch), device_id_type=MESH,
        )

    def cot_arrival(source):
        return pltpu.make_async_remote_copy(
            src_ref=stage.at[pl.ds(source * 2, 2)], dst_ref=cotf.at[col, source],
            send_sem=cs.at[source], recv_sem=cr.at[source],
            device_id=(row, col, ch), device_id_type=MESH,
        )

    def x_copy(block, r, sems, recvs, side, there):
        return pltpu.make_async_remote_copy(
            src_ref=cotf.at[block, r], dst_ref=cotf.at[block, r],
            send_sem=sems.at[r, side], recv_sem=recvs.at[r, side],
            device_id=(row, there, ch), device_id_type=MESH,
        )

    def x_relay(block, r, side, there):
        return pltpu.make_async_remote_copy(
            src_ref=cotf.at[block, r, side], dst_ref=cotf.at[block, r, side],
            send_sem=fs.at[r, side], recv_sem=fr.at[r, side],
            device_id=(row, there, ch), device_id_type=MESH,
        )

    blocks = [row]
    for step in (6, 5, 7, 2, 4, 1, 3):
        z_lo = (row // 4 + step // 4) % 2
        cot_copy(z_lo * 4 + (row + step) % 4).start()
        blocks.append(z_lo * 4 + (row + 8 - step) % 4)
    cotf[col, row] = stage[pl.ds(row * 2, 2)]

    def x_send(n):
        r = blocks[n]
        if n > 0:
            cot_arrival(r).wait_recv()
        x_copy(col, r, xs, xr, 0, east).start()
        x_copy(col, r, xs, xr, 1, west).start()

    def x_forward(n):
        r = blocks[n]
        x_copy(west, r, xs, xr, 0, east).wait_recv()
        x_relay(west, r, 0, east).start()
        x_copy(east, r, xs, xr, 1, west).wait_recv()
        x_relay(east, r, 1, west).start()

    def x_finish(n):
        r = blocks[n]
        x_relay(far, r, 0, east).wait_recv()
        x_relay(far, r, 1, west).wait_recv()

    x_send(0)

    def to_owners():
        for kind, t, side in GROUPS:
            owned[owner_row(kind, t, side):owner_row(kind, t, side) + 4] = natural[
                stream_row(kind, t, side):stream_row(kind, t, side) + 4
            ]

    def to_streams():
        for kind, t, side in GROUPS:
            natural[stream_row(kind, t, side):stream_row(kind, t, side) + 4] = owned[
                owner_row(kind, t, side):owner_row(kind, t, side) + 4
            ]

    for s in range(4):
        natural[s * 128:(s + 1) * 128] = weight_ref[:, s * 128:(s + 1) * 128].astype(F32).T
    to_owners()
    wt_ref[...] = owned[...].astype(BF16)
    for s in range(4):
        wb_ref[:, s * 128:(s + 1) * 128] = owned[s * 128:(s + 1) * 128].T.astype(BF16)
    for s in range(4):
        natural[s * 128:(s + 1) * 128] = jnp.broadcast_to(biases_ref[s:s + 1], (128, 128)).T
    to_owners()
    for half in range(2):
        lanes = slice(half * 128, (half + 1) * 128)
        bias_ref[:, lanes] = owned[...]
        gain_ref[:, lanes] = jnp.broadcast_to(gains_ref[...], (128, 128)).T
        shift_ref[:, lanes] = jnp.broadcast_to(shifts_ref[...], (128, 128)).T

    left[...] = jnp.zeros_like(left)
    for p in range(2):
        for x in range(4):
            right[p, x, COLS:256] = jnp.zeros((16, 256), BF16)
    acc[...] = jnp.zeros_like(acc)
    small[...] = jnp.zeros_like(small)
    acc_gain[...] = jnp.zeros_like(acc_gain)
    acc_shift[...] = jnp.zeros_like(acc_shift)

    def forward(kh, ip, carry):
        width = HALF_COLS[kh]
        tokens = []
        for half in range(2):
            x = pair_ref[2 * ip + half, kh * 128:kh * 128 + width].astype(F32)
            if width < 128:
                x = jnp.concatenate([x, jnp.zeros((128 - width, 128), F32)], axis=0)
            tokens.append(x.T)
        x = jnp.concatenate(tokens, axis=1)
        centred = x - jnp.mean(x, axis=0, keepdims=True)
        inv_std = lax.rsqrt(jnp.mean(centred * centred, axis=0, keepdims=True) + EPSILON)
        scaled = centred * inv_std
        normed = (scaled * gain_ref[...] + shift_ref[...]).astype(BF16)
        slot = kh * PAIRS + ip
        scaled_s[slot] = scaled
        inv_s[slot] = inv_std
        normed_s[slot, 0:128] = normed
        normed_s[slot, 128:144] = jnp.ones((16, 256), BF16)
        linear = jnp.dot(wt_ref[...], normed, preferred_element_type=F32) + bias_ref[...]
        gate = 0.5 * jnp.tanh(0.5 * linear[0:256]) + 0.5
        side = gate * linear[256:512]
        if width < 128:
            lane = lax.broadcasted_iota(jnp.int32, (256, 256), 1)
            side = jnp.where(lane % 128 < width, side, 0.0)
        packed = jnp.concatenate(
            [side[:, 0:128].reshape(OWNERS, 8, 128), side[:, 128:256].reshape(OWNERS, 8, 128)], axis=1
        ).astype(BF16)
        send1[kh, :, pl.ds(pl.multiple_of(ip * 16, 16), 16), :] = packed
        return carry

    def exchange(source, target, send_sem, recv_sem, kh, there_r, there_g):
        there = there_r * 4 + there_g
        return pltpu.make_async_remote_copy(
            src_ref=source.at[kh, there], dst_ref=target.at[kh, me],
            send_sem=send_sem.at[kh, there], recv_sem=recv_sem.at[kh, me],
            device_id=(there_r, col, there_g), device_id_type=MESH,
        )

    def arrival(source, target, send_sem, recv_sem, kh, there):
        return pltpu.make_async_remote_copy(
            src_ref=source.at[kh, there], dst_ref=target.at[kh, there],
            send_sem=send_sem.at[kh, there], recv_sem=recv_sem.at[kh, there],
            device_id=(row, col, ch), device_id_type=MESH,
        )

    def send_all(source, target, send_sem, recv_sem, kh):
        for r, g in partners:
            exchange(source, target, send_sem, recv_sem, kh, r, g).start()
        target[kh, me] = source[kh, me]

    def others(action):
        def one(there, carry):
            @pl.when(there != me)
            def _():
                action(there)
            return carry

        lax.fori_loop(0, OWNERS, one, 0)

    def regroup(kh):
        others(lambda there: arrival(send1, recv1, s1, r1, kh, there).wait_recv())

        def widen(source, carry):
            wide[pl.ds(pl.multiple_of(source * 240, 8), 240)] = recv1[kh, source].astype(F32)
            return carry

        lax.fori_loop(0, OWNERS, widen, 0)
        for p in range(2):
            for q in range(2):
                lanes = slice(q * 128, q * 128 + 128)
                for r in range(8):
                    left[p, r, q * 120:q * 120 + 120, lanes] = wide[
                        pl.ds(r * 960 + 2 * p + q, 120, stride=8)
                    ].astype(BF16)
                for x in range(4):
                    right[p, x, 0:COLS, lanes] = wide[
                        pl.ds(x * 1920 + 4 + 2 * p + q, COLS, stride=8)
                    ].astype(BF16)

    def triangle(group, first):
        for n in group:
            r = blocks[n]
            for p in range(2):
                total = jnp.dot(cotf[0, r, p], right[p, 0], preferred_element_type=F32)
                for x in range(1, 4):
                    total += jnp.dot(cotf[x, r, p], right[p, x], preferred_element_type=F32)
                for q in range(2):
                    wide[pl.ds(r * 960 + 2 * p + q, 120, stride=8)] = total[
                        q * 120:q * 120 + 120, q * 128:q * 128 + 128
                    ]
        for p in range(2):
            for x in range(4):
                total = None
                for n in group:
                    term = lax.dot_general(
                        cotf[x, blocks[n], p], left[p, blocks[n]], (((0,), (0,)), ((), ())),
                        preferred_element_type=F32,
                    )
                    total = term if total is None else total + term
                for q in range(2):
                    rows = pl.ds(x * 1920 + 4 + 2 * p + q, COLS, stride=8)
                    part = total[0:COLS, q * 128:q * 128 + 128]
                    wide[rows] = part if first else wide[rows] + part

    def give_back(kh):
        def narrow(target, carry):
            send2[kh, target] = wide[pl.ds(pl.multiple_of(target * 240, 8), 240)].astype(BF16)
            return carry

        lax.fori_loop(0, OWNERS, narrow, 0)
        for n in BACK[kh]:
            for r, g in partners:
                back_copy(n, r * 4 + g, me, r, g).start()
        recv2[kh, me] = send2[kh, me]

    def back_copy(n, source, target, r, g):
        kh, start, stop = BACK_CHUNKS[n]
        rows = pl.ds(start * 16, (stop - start) * 16)
        return pltpu.make_async_remote_copy(
            src_ref=send2.at[kh, source, rows], dst_ref=recv2.at[kh, target, rows],
            send_sem=s2.at[n, source], recv_sem=r2.at[n, target],
            device_id=(r, col, g), device_id_type=MESH,
        )

    def backward(kh, ip, carry):
        width = HALF_COLS[kh]
        slot = kh * PAIRS + ip
        back = recv2[kh, :, pl.ds(pl.multiple_of(ip * 16, 16), 16), :].astype(F32)
        side_grad = jnp.concatenate(
            [back[:, 0:8].reshape(256, 128), back[:, 8:16].reshape(256, 128)], axis=1
        )
        normed = normed_s[slot, 0:128]
        linear = jnp.dot(wt_ref[...], normed, preferred_element_type=F32) + bias_ref[...]
        gate = 0.5 * jnp.tanh(0.5 * linear[0:256]) + 0.5
        value_grad = side_grad * gate
        gate_grad = value_grad * linear[256:512] * (1.0 - gate)
        linear_grad = jnp.concatenate([gate_grad.astype(BF16), value_grad.astype(BF16)], axis=0)
        normed_grad = jnp.dot(wb_ref[...], linear_grad, preferred_element_type=F32)
        acc[...] += lax.dot_general(
            normed_s[slot], linear_grad, (((1,), (1,)), ((), ())), preferred_element_type=F32
        )
        scaled = scaled_s[slot]
        acc_gain[...] += normed_grad * scaled
        acc_shift[...] += normed_grad
        gained = normed_grad * gain_ref[...]
        centre = jnp.mean(gained, axis=0, keepdims=True)
        slope = jnp.mean(gained * scaled, axis=0, keepdims=True)
        result = (gained - centre - scaled * slope) * inv_s[slot]
        for half in range(2):
            out = result[:, half * 128:(half + 1) * 128].T.astype(BF16)
            grad_ref[2 * ip + half, kh * 128:kh * 128 + width] = out[0:width]
        return carry

    lax.fori_loop(0, 8, functools.partial(forward, 0), 0)
    x_send(1)
    lax.fori_loop(8, PAIRS, functools.partial(forward, 0), 0)
    send_all(send1, recv1, s1, r1, 0)
    x_send(2)
    x_forward(0)
    lax.fori_loop(0, 5, functools.partial(forward, 1), 0)
    x_send(3)
    x_forward(1)
    lax.fori_loop(5, 10, functools.partial(forward, 1), 0)
    x_send(4)
    x_forward(2)
    lax.fori_loop(10, PAIRS, functools.partial(forward, 1), 0)
    send_all(send1, recv1, s1, r1, 1)
    x_send(5)
    x_forward(3)
    x_send(6)
    x_forward(4)
    x_send(7)
    x_forward(5)
    regroup(0)
    x_forward(6)
    for n in range(6):
        x_finish(n)
    triangle(range(0, 6), True)
    x_forward(7)
    x_finish(6)
    x_finish(7)
    triangle(range(6, 8), False)
    give_back(0)
    regroup(1)
    triangle(range(0, 8), True)
    give_back(1)
    for n, (kh, start, stop) in enumerate(BACK_CHUNKS):
        others(lambda there: back_copy(n, there, there, row, ch).wait_recv())
        lax.fori_loop(start, stop, functools.partial(backward, kh), 0)

    for s in range(4):
        small[s:s + 1] = acc[128:129, s * 128:(s + 1) * 128]
    small[4:5] = jnp.sum(acc_gain[...].T, axis=0, keepdims=True)
    small[5:6] = jnp.sum(acc_shift[...].T, axis=0, keepdims=True)
    for o in range(OWNERS):
        rows, lane = slice((o // 2) * 8, (o // 2) * 8 + 8), (o % 2) * 256
        part_s[o, 0:8] = acc[rows, lane:lane + 128]
        part_s[o, 8:16] = acc[rows, lane + 128:lane + 256]
        part_s[o, 16:24] = small[...]
    for r, g in partners:
        there = r * 4 + g
        pltpu.make_async_remote_copy(
            src_ref=part_s.at[there], dst_ref=part_r.at[me], send_sem=as_.at[there], recv_sem=ar.at[me],
            device_id=(r, col, g), device_id_type=MESH,
        ).start()
    part_r[me] = part_s[me]

    def part_arrival(there):
        return pltpu.make_async_remote_copy(
            src_ref=part_s.at[there], dst_ref=part_r.at[there], send_sem=as_.at[there], recv_sem=ar.at[there],
            device_id=(row, col, ch), device_id_type=MESH,
        )

    others(lambda there: part_arrival(there).wait_recv())
    total = part_r[0]
    for o in range(1, OWNERS):
        total = total + part_r[o]
    line[col] = total

    def line_copy(slot, there):
        return pltpu.make_async_remote_copy(
            src_ref=line.at[slot], dst_ref=line.at[slot], send_sem=bs.at[there], recv_sem=br.at[slot],
            device_id=(row, there, ch), device_id_type=MESH,
        )

    for there in (far, east, west):
        line_copy(col, there).start()
    for there in (far, east, west):
        line_copy(there, there).wait_recv()
    total = (line[0] + line[1]) + (line[2] + line[3])
    total = total * (1.0 / CROP)
    whole[me] = total[0:16]
    small_ref[...] = total[16:24]

    def whole_copy(slot, there, r, g):
        return pltpu.make_async_remote_copy(
            src_ref=whole.at[slot], dst_ref=whole.at[slot], send_sem=gs_.at[there], recv_sem=gr.at[slot],
            device_id=(r, col, g), device_id_type=MESH,
        )

    for r, g in partners:
        whole_copy(me, r * 4 + g, r, g).start()
    others(lambda there: whole_copy(there, there, row, ch).wait_recv())
    for o in range(OWNERS):
        rows, lane = slice((o // 2) * 8, (o // 2) * 8 + 8), (o % 2) * 256
        acc[rows, lane:lane + 128] = whole[o, 0:8]
        acc[rows, lane + 128:lane + 256] = whole[o, 8:16]
    for s in range(4):
        owned[s * 128:(s + 1) * 128] = acc[0:128, s * 128:(s + 1) * 128].T
    to_streams()
    for s in range(4):
        dw_ref[:, s * 128:(s + 1) * 128] = natural[s * 128:(s + 1) * 128].T
    for s in range(4):
        owned[s * 128:(s + 1) * 128] = jnp.broadcast_to(small_ref[s:s + 1], (128, 128)).T
    to_streams()
    for s in range(4):
        small_ref[s:s + 1] = natural[s * 128:(s + 1) * 128].T[0:1]

    others(lambda there: part_arrival(there).wait_send())
    others(lambda there: whole_copy(me, there, row, ch).wait_send())
    for there in (far, east, west):
        line_copy(col, there).wait_send()
    for n in range(8):
        r = blocks[n]
        if n > 0:
            cot_copy(r).wait_send()
        x_copy(col, r, xs, xr, 0, east).wait_send()
        x_copy(col, r, xs, xr, 1, west).wait_send()
        x_relay(west, r, 0, east).wait_send()
        x_relay(east, r, 1, west).wait_send()
    for kh in range(2):
        others(lambda there: arrival(send1, recv1, s1, r1, kh, there).wait_send())
    for n in range(len(BACK_CHUNKS)):
        others(lambda there: back_copy(n, there, there, row, ch).wait_send())


def shards(pair, norm_gain, norm_shift, proj_weight, proj_bias, prod_cot):
    vmem = pl.BlockSpec(memory_space=pltpu.VMEM)
    dma = pltpu.SemaphoreType.DMA
    grad_pair, dw, small = pl.pallas_call(
        kernel,
        out_shape=(
            jax.ShapeDtypeStruct((ROWS, COLS, 128), BF16),
            jax.ShapeDtypeStruct((128, 512), F32),
            jax.ShapeDtypeStruct((8, 128), F32),
        ),
        in_specs=[vmem] * 6,
        out_specs=(vmem,) * 3,
        scratch_shapes=[
            pltpu.VMEM((16, 240, 256), BF16),
            pltpu.VMEM((4, 8, 2, 240, 256), BF16),
            pltpu.VMEM((2, OWNERS, 240, 128), BF16),
            pltpu.VMEM((2, OWNERS, 240, 128), BF16),
            pltpu.VMEM((2, 8, 240, 256), BF16),
            pltpu.VMEM((2, 4, 256, 256), BF16),
            pltpu.VMEM((CROP * 8, 128), F32),
            pltpu.VMEM((2, OWNERS, 240, 128), BF16),
            pltpu.VMEM((2, OWNERS, 240, 128), BF16),
            pltpu.VMEM((2 * PAIRS, 128, 256), F32),
            pltpu.VMEM((2 * PAIRS, 1, 256), F32),
            pltpu.VMEM((2 * PAIRS, 144, 256), BF16),
            pltpu.VMEM((128, 256), F32),
            pltpu.VMEM((128, 256), F32),
            pltpu.VMEM((512, 128), BF16),
            pltpu.VMEM((128, 512), BF16),
            pltpu.VMEM((512, 256), F32),
            pltpu.VMEM((128, 256), F32),
            pltpu.VMEM((128, 256), F32),
            pltpu.VMEM((512, 128), F32),
            pltpu.VMEM((512, 128), F32),
            pltpu.VMEM((144, 512), F32),
            pltpu.VMEM((8, 128), F32),
            pltpu.VMEM((OWNERS, 24, 128), F32),
            pltpu.VMEM((OWNERS, 24, 128), F32),
            pltpu.VMEM((4, 24, 128), F32),
            pltpu.VMEM((OWNERS, 16, 128), F32),
            dma((8,)), dma((8,)), dma((8, 2)), dma((8, 2)), dma((8, 2)), dma((8, 2)),
            dma((2, OWNERS)), dma((2, OWNERS)), dma((3, OWNERS)), dma((3, OWNERS)),
            dma((OWNERS,)), dma((OWNERS,)), dma((4,)), dma((4,)), dma((OWNERS,)), dma((OWNERS,)),
        ],
        compiler_params=pltpu.CompilerParams(
            collective_id=0, has_side_effects=True, vmem_limit_bytes=60 << 20
        ),
        name="triangle_backward",
    )(pair, prod_cot, proj_weight.reshape(128, 512), proj_bias, norm_gain.reshape(1, 128), norm_shift.reshape(1, 128))
    return grad_pair, dw.reshape(128, 4, 128), small[0:4], small[4], small[5]


def solution(mesh):
    in_specs = (P(("row", "ch"), "col", None), P(), P(), P(), P(), P("ch", "row", "col"))
    out_specs = (P(("row", "ch"), "col", None), P(), P(), P(), P())
    return jax.shard_map(shards, mesh=mesh, in_specs=in_specs, out_specs=out_specs, check_vma=False)
```

```python
import functools

import jax
import jax.numpy as jnp
from jax import lax
from jax.experimental import pallas as pl
from jax.experimental.pallas import tpu as pltpu
from jax.sharding import PartitionSpec as P

MESH = pl.DeviceIdType.MESH
EPSILON = 1e-05
CROP = 960
ROWS = 30
COLS = 240
PAIRS = ROWS // 2
HALF_COLS = (128, COLS - 128)
OWNERS = 32
F32, BF16 = jnp.float32, jnp.bfloat16

STEPS = (
    (2, 2),
    (1, 1), (3, 3), (1, 3), (3, 1),
    (1, 2), (2, 1), (3, 2), (2, 3),
    (2, 0), (0, 2),
    (1, 0), (0, 1), (3, 0), (0, 3),
)
OFFSETS = [(dz, dy, core) for core in range(2) for dz, dy in STEPS] + [(0, 0, 1)]


BACK_CHUNKS = ((0, 0, PAIRS), (1, 0, 8), (1, 8, PAIRS))
BACK = ((0,), (1, 2))
GROUPS = [(kind, t, side) for kind in range(2) for t in range(OWNERS) for side in range(2)]


def owner_row(kind, t, side):
    return kind * 256 + t * 8 + side * 4


def stream_row(kind, t, side):
    return (side * 2 + kind) * 128 + (t % 4) * 32 + (t // 4) * 4


def kernel(
    pair_ref, cot_ref, weight_ref, biases_ref, gains_ref, shifts_ref,
    grad_ref, dw_ref, small_ref,
    stage, cotf, send1, recv1, left, right, wide, send2, recv2, scaled_s, inv_s, normed_s, acc_gain, acc_shift,
    wt_ref, wb_ref, bias_ref, gain_ref, shift_ref, natural, owned, acc, small, part_s, part_r, line, whole,
    cs, cr, xs, xr, fs, fr, s1, r1, s2, r2, as_, ar, bs, br, gs_, gr,
):
    row, col, ch = lax.axis_index("row"), lax.axis_index("col"), lax.axis_index("ch")
    me = row * 4 + ch
    z = (ch // 2) * 2 + row // 4
    y = row % 4
    core = ch % 2
    east, west, far = (col + 1) % 4, (col + 3) % 4, (col + 2) % 4

    partners = []
    for dz, dy, dk in OFFSETS:
        z2, y2, k2 = (z + dz) % 4, (y + dy) % 4, (core + dk) % 2
        partners.append(((z2 % 2) * 4 + y2, (z2 // 2) * 2 + k2))

    barrier = pltpu.get_barrier_semaphore()
    for r, g in partners:
        pl.semaphore_signal(barrier, 1, device_id=(r, col, g), device_id_type=MESH)
    for c in (east, west, far):
        pl.semaphore_signal(barrier, 1, device_id=(row, c, ch), device_id_type=MESH)

    def stage_one(pair, carry):
        stage[pair] = jnp.zeros((240, 256), BF16)
        stage[pair, 0:120, 0:COLS] = cot_ref[2 * pair]
        stage[pair, 120:240, 0:COLS] = cot_ref[2 * pair + 1]
        return carry

    lax.fori_loop(0, 16, stage_one, 0)
    pl.semaphore_wait(barrier, len(partners) + 3)

    def cot_copy(there):
        return pltpu.make_async_remote_copy(
            src_ref=stage.at[pl.ds(there * 2, 2)], dst_ref=cotf.at[col, row],
            send_sem=cs.at[there], recv_sem=cr.at[row],
            device_id=(there, col, ch), device_id_type=MESH,
        )

    def cot_arrival(source):
        return pltpu.make_async_remote_copy(
            src_ref=stage.at[pl.ds(source * 2, 2)], dst_ref=cotf.at[col, source],
            send_sem=cs.at[source], recv_sem=cr.at[source],
            device_id=(row, col, ch), device_id_type=MESH,
        )

    def x_copy(block, r, sems, recvs, side, there):
        return pltpu.make_async_remote_copy(
            src_ref=cotf.at[block, r], dst_ref=cotf.at[block, r],
            send_sem=sems.at[r, side], recv_sem=recvs.at[r, side],
            device_id=(row, there, ch), device_id_type=MESH,
        )

    def x_relay(block, r, side, there):
        return pltpu.make_async_remote_copy(
            src_ref=cotf.at[block, r, side], dst_ref=cotf.at[block, r, side],
            send_sem=fs.at[r, side], recv_sem=fr.at[r, side],
            device_id=(row, there, ch), device_id_type=MESH,
        )

    blocks = [row]
    for step in (6, 5, 7, 2, 4, 1, 3):
        z_lo = (row // 4 + step // 4) % 2
        cot_copy(z_lo * 4 + (row + step) % 4).start()
        blocks.append(z_lo * 4 + (row + 8 - step) % 4)
    cotf[col, row] = stage[pl.ds(row * 2, 2)]

    def x_send(n):
        r = blocks[n]
        if n > 0:
            cot_arrival(r).wait_recv()
        x_copy(col, r, xs, xr, 0, east).start()
        x_copy(col, r, xs, xr, 1, west).start()

    def x_forward(n):
        r = blocks[n]
        x_copy(west, r, xs, xr, 0, east).wait_recv()
        x_relay(west, r, 0, east).start()
        x_copy(east, r, xs, xr, 1, west).wait_recv()
        x_relay(east, r, 1, west).start()

    def x_finish(n):
        r = blocks[n]
        x_relay(far, r, 0, east).wait_recv()
        x_relay(far, r, 1, west).wait_recv()

    x_send(0)

    def to_owners():
        for kind, t, side in GROUPS:
            owned[owner_row(kind, t, side):owner_row(kind, t, side) + 4] = natural[
                stream_row(kind, t, side):stream_row(kind, t, side) + 4
            ]

    def to_streams():
        for kind, t, side in GROUPS:
            natural[stream_row(kind, t, side):stream_row(kind, t, side) + 4] = owned[
                owner_row(kind, t, side):owner_row(kind, t, side) + 4
            ]

    weights = weight_ref[...].astype(F32)
    for s in range(4):
        natural[s * 128:(s + 1) * 128] = weights[:, s, :].T
    to_owners()
    wt_ref[...] = owned[...].astype(BF16)
    for s in range(4):
        wb_ref[:, s * 128:(s + 1) * 128] = owned[s * 128:(s + 1) * 128].T.astype(BF16)
    for s in range(4):
        natural[s * 128:(s + 1) * 128] = jnp.broadcast_to(biases_ref[s:s + 1], (128, 128)).T
    to_owners()
    for half in range(2):
        lanes = slice(half * 128, (half + 1) * 128)
        bias_ref[:, lanes] = owned[...]
        gain_ref[:, lanes] = jnp.broadcast_to(gains_ref[...], (128, 128)).T
        shift_ref[:, lanes] = jnp.broadcast_to(shifts_ref[...], (128, 128)).T

    left[...] = jnp.zeros_like(left)
    for p in range(2):
        for x in range(4):
            right[p, x, COLS:256] = jnp.zeros((16, 256), BF16)
    acc[...] = jnp.zeros_like(acc)
    small[...] = jnp.zeros_like(small)
    acc_gain[...] = jnp.zeros_like(acc_gain)
    acc_shift[...] = jnp.zeros_like(acc_shift)

    def forward(kh, ip, carry):
        width = HALF_COLS[kh]
        tokens = []
        for half in range(2):
            x = pair_ref[2 * ip + half, kh * 128:kh * 128 + width].astype(F32)
            if width < 128:
                x = jnp.concatenate([x, jnp.zeros((128 - width, 128), F32)], axis=0)
            tokens.append(x.T)
        x = jnp.concatenate(tokens, axis=1)
        centred = x - jnp.mean(x, axis=0, keepdims=True)
        inv_std = lax.rsqrt(jnp.mean(centred * centred, axis=0, keepdims=True) + EPSILON)
        scaled = centred * inv_std
        normed = (scaled * gain_ref[...] + shift_ref[...]).astype(BF16)
        slot = kh * PAIRS + ip
        scaled_s[slot] = scaled
        inv_s[slot] = inv_std
        normed_s[slot, 0:128] = normed
        normed_s[slot, 128:144] = jnp.ones((16, 256), BF16)
        linear = jnp.dot(wt_ref[...], normed, preferred_element_type=F32) + bias_ref[...]
        gate = 0.5 * jnp.tanh(0.5 * linear[0:256]) + 0.5
        side = gate * linear[256:512]
        if width < 128:
            lane = lax.broadcasted_iota(jnp.int32, (256, 256), 1)
            side = jnp.where(lane % 128 < width, side, 0.0)
        packed = jnp.concatenate(
            [side[:, 0:128].reshape(OWNERS, 8, 128), side[:, 128:256].reshape(OWNERS, 8, 128)], axis=1
        ).astype(BF16)
        send1[kh, :, pl.ds(pl.multiple_of(ip * 16, 16), 16), :] = packed
        return carry

    def exchange(source, target, send_sem, recv_sem, kh, there_r, there_g):
        there = there_r * 4 + there_g
        return pltpu.make_async_remote_copy(
            src_ref=source.at[kh, there], dst_ref=target.at[kh, me],
            send_sem=send_sem.at[kh, there], recv_sem=recv_sem.at[kh, me],
            device_id=(there_r, col, there_g), device_id_type=MESH,
        )

    def arrival(source, target, send_sem, recv_sem, kh, there):
        return pltpu.make_async_remote_copy(
            src_ref=source.at[kh, there], dst_ref=target.at[kh, there],
            send_sem=send_sem.at[kh, there], recv_sem=recv_sem.at[kh, there],
            device_id=(row, col, ch), device_id_type=MESH,
        )

    def send_all(source, target, send_sem, recv_sem, kh):
        for r, g in partners:
            exchange(source, target, send_sem, recv_sem, kh, r, g).start()
        target[kh, me] = source[kh, me]

    def others(action):
        def one(there, carry):
            @pl.when(there != me)
            def _():
                action(there)
            return carry

        lax.fori_loop(0, OWNERS, one, 0)

    def regroup(kh):
        others(lambda there: arrival(send1, recv1, s1, r1, kh, there).wait_recv())

        def widen(source, carry):
            wide[pl.ds(pl.multiple_of(source * 240, 8), 240)] = recv1[kh, source].astype(F32)
            return carry

        lax.fori_loop(0, OWNERS, widen, 0)
        for p in range(2):
            for q in range(2):
                lanes = slice(q * 128, q * 128 + 128)
                for r in range(8):
                    left[p, r, q * 120:q * 120 + 120, lanes] = wide[
                        pl.ds(r * 960 + 2 * p + q, 120, stride=8)
                    ].astype(BF16)
                for x in range(4):
                    right[p, x, 0:COLS, lanes] = wide[
                        pl.ds(x * 1920 + 4 + 2 * p + q, COLS, stride=8)
                    ].astype(BF16)

    def triangle(group, first):
        for n in group:
            r = blocks[n]
            for p in range(2):
                total = jnp.dot(cotf[0, r, p], right[p, 0], preferred_element_type=F32)
                for x in range(1, 4):
                    total += jnp.dot(cotf[x, r, p], right[p, x], preferred_element_type=F32)
                for q in range(2):
                    wide[pl.ds(r * 960 + 2 * p + q, 120, stride=8)] = total[
                        q * 120:q * 120 + 120, q * 128:q * 128 + 128
                    ]
        for p in range(2):
            for x in range(4):
                total = None
                for n in group:
                    term = lax.dot_general(
                        cotf[x, blocks[n], p], left[p, blocks[n]], (((0,), (0,)), ((), ())),
                        preferred_element_type=F32,
                    )
                    total = term if total is None else total + term
                for q in range(2):
                    rows = pl.ds(x * 1920 + 4 + 2 * p + q, COLS, stride=8)
                    part = total[0:COLS, q * 128:q * 128 + 128]
                    wide[rows] = part if first else wide[rows] + part

    def give_back(kh):
        def narrow(target, carry):
            send2[kh, target] = wide[pl.ds(pl.multiple_of(target * 240, 8), 240)].astype(BF16)
            return carry

        lax.fori_loop(0, OWNERS, narrow, 0)
        for n in BACK[kh]:
            for r, g in partners:
                back_copy(n, r * 4 + g, me, r, g).start()
        recv2[kh, me] = send2[kh, me]

    def back_copy(n, source, target, r, g):
        kh, start, stop = BACK_CHUNKS[n]
        rows = pl.ds(start * 16, (stop - start) * 16)
        return pltpu.make_async_remote_copy(
            src_ref=send2.at[kh, source, rows], dst_ref=recv2.at[kh, target, rows],
            send_sem=s2.at[n, source], recv_sem=r2.at[n, target],
            device_id=(r, col, g), device_id_type=MESH,
        )

    def backward(kh, ip, carry):
        width = HALF_COLS[kh]
        slot = kh * PAIRS + ip
        back = recv2[kh, :, pl.ds(pl.multiple_of(ip * 16, 16), 16), :].astype(F32)
        side_grad = jnp.concatenate(
            [back[:, 0:8].reshape(256, 128), back[:, 8:16].reshape(256, 128)], axis=1
        )
        normed = normed_s[slot, 0:128]
        linear = jnp.dot(wt_ref[...], normed, preferred_element_type=F32) + bias_ref[...]
        gate = 0.5 * jnp.tanh(0.5 * linear[0:256]) + 0.5
        value_grad = side_grad * gate
        gate_grad = value_grad * linear[256:512] * (1.0 - gate)
        linear_grad = jnp.concatenate([gate_grad.astype(BF16), value_grad.astype(BF16)], axis=0)
        normed_grad = jnp.dot(wb_ref[...], linear_grad, preferred_element_type=F32)
        acc[...] += lax.dot_general(
            normed_s[slot], linear_grad, (((1,), (1,)), ((), ())), preferred_element_type=F32
        )
        scaled = scaled_s[slot]
        acc_gain[...] += normed_grad * scaled
        acc_shift[...] += normed_grad
        gained = normed_grad * gain_ref[...]
        centre = jnp.mean(gained, axis=0, keepdims=True)
        slope = jnp.mean(gained * scaled, axis=0, keepdims=True)
        result = (gained - centre - scaled * slope) * inv_s[slot]
        for half in range(2):
            out = result[:, half * 128:(half + 1) * 128].T.astype(BF16)
            grad_ref[2 * ip + half, kh * 128:kh * 128 + width] = out[0:width]
        return carry

    lax.fori_loop(0, 8, functools.partial(forward, 0), 0)
    x_send(1)
    lax.fori_loop(8, PAIRS, functools.partial(forward, 0), 0)
    send_all(send1, recv1, s1, r1, 0)
    x_send(2)
    x_forward(0)
    lax.fori_loop(0, 5, functools.partial(forward, 1), 0)
    x_send(3)
    x_forward(1)
    lax.fori_loop(5, 10, functools.partial(forward, 1), 0)
    x_send(4)
    x_forward(2)
    lax.fori_loop(10, PAIRS, functools.partial(forward, 1), 0)
    send_all(send1, recv1, s1, r1, 1)
    x_send(5)
    x_forward(3)
    x_send(6)
    x_forward(4)
    x_send(7)
    x_forward(5)
    regroup(0)
    x_forward(6)
    for n in range(6):
        x_finish(n)
    triangle(range(0, 6), True)
    x_forward(7)
    x_finish(6)
    x_finish(7)
    triangle(range(6, 8), False)
    give_back(0)
    regroup(1)
    triangle(range(0, 8), True)
    give_back(1)
    for n, (kh, start, stop) in enumerate(BACK_CHUNKS):
        others(lambda there: back_copy(n, there, there, row, ch).wait_recv())
        lax.fori_loop(start, stop, functools.partial(backward, kh), 0)

    for s in range(4):
        small[s:s + 1] = acc[128:129, s * 128:(s + 1) * 128]
    small[4:5] = jnp.sum(acc_gain[...].T, axis=0, keepdims=True)
    small[5:6] = jnp.sum(acc_shift[...].T, axis=0, keepdims=True)
    coarse = small[...].astype(BF16)
    fine = small[...] - coarse.astype(F32)
    small_parts = jnp.concatenate([coarse.astype(F32), fine], axis=0).astype(BF16)
    for o in range(OWNERS):
        rows, lane = slice((o // 2) * 8, (o // 2) * 8 + 8), (o % 2) * 256
        part_s[o, 0:16] = jnp.concatenate(
            [acc[rows, lane:lane + 128], acc[rows, lane + 128:lane + 256]], axis=0
        ).astype(BF16)
        part_s[o, 16:32] = small_parts
    for r, g in partners:
        there = r * 4 + g
        pltpu.make_async_remote_copy(
            src_ref=part_s.at[there], dst_ref=part_r.at[me], send_sem=as_.at[there], recv_sem=ar.at[me],
            device_id=(r, col, g), device_id_type=MESH,
        ).start()
    part_r[me] = part_s[me]

    def part_arrival(there):
        return pltpu.make_async_remote_copy(
            src_ref=part_s.at[there], dst_ref=part_r.at[there], send_sem=as_.at[there], recv_sem=ar.at[there],
            device_id=(row, col, ch), device_id_type=MESH,
        )

    others(lambda there: part_arrival(there).wait_recv())
    total = part_r[0].astype(F32)
    for o in range(1, OWNERS):
        total = total + part_r[o].astype(F32)
    line[col, 0:16] = total[0:16]
    line[col, 16:24] = total[16:24] + total[24:32]

    def line_copy(slot, there):
        return pltpu.make_async_remote_copy(
            src_ref=line.at[slot], dst_ref=line.at[slot], send_sem=bs.at[there], recv_sem=br.at[slot],
            device_id=(row, there, ch), device_id_type=MESH,
        )

    for there in (far, east, west):
        line_copy(col, there).start()
    for there in (far, east, west):
        line_copy(there, there).wait_recv()
    total = (line[0] + line[1]) + (line[2] + line[3])
    total = total * (1.0 / CROP)
    whole[me] = total[0:16]
    small_ref[...] = total[16:24]

    def whole_copy(slot, there, r, g):
        return pltpu.make_async_remote_copy(
            src_ref=whole.at[slot], dst_ref=whole.at[slot], send_sem=gs_.at[there], recv_sem=gr.at[slot],
            device_id=(r, col, g), device_id_type=MESH,
        )

    for r, g in partners:
        whole_copy(me, r * 4 + g, r, g).start()
    others(lambda there: whole_copy(there, there, row, ch).wait_recv())
    for o in range(OWNERS):
        rows, lane = slice((o // 2) * 8, (o // 2) * 8 + 8), (o % 2) * 256
        acc[rows, lane:lane + 128] = whole[o, 0:8]
        acc[rows, lane + 128:lane + 256] = whole[o, 8:16]
    for s in range(4):
        owned[s * 128:(s + 1) * 128] = acc[0:128, s * 128:(s + 1) * 128].T
    to_streams()
    for s in range(4):
        dw_ref[:, s, :] = natural[s * 128:(s + 1) * 128].T
    for s in range(4):
        owned[s * 128:(s + 1) * 128] = jnp.broadcast_to(small_ref[s:s + 1], (128, 128)).T
    to_streams()
    for s in range(4):
        small_ref[s:s + 1] = natural[s * 128:(s + 1) * 128].T[0:1]

    others(lambda there: part_arrival(there).wait_send())
    others(lambda there: whole_copy(me, there, row, ch).wait_send())
    for there in (far, east, west):
        line_copy(col, there).wait_send()
    for n in range(8):
        r = blocks[n]
        if n > 0:
            cot_copy(r).wait_send()
        x_copy(col, r, xs, xr, 0, east).wait_send()
        x_copy(col, r, xs, xr, 1, west).wait_send()
        x_relay(west, r, 0, east).wait_send()
        x_relay(east, r, 1, west).wait_send()
    for kh in range(2):
        others(lambda there: arrival(send1, recv1, s1, r1, kh, there).wait_send())
    for n in range(len(BACK_CHUNKS)):
        others(lambda there: back_copy(n, there, there, row, ch).wait_send())


def shards(pair, norm_gain, norm_shift, proj_weight, proj_bias, prod_cot):
    vmem = pl.BlockSpec(memory_space=pltpu.VMEM)
    dma = pltpu.SemaphoreType.DMA
    grad_pair, dw, small = pl.pallas_call(
        kernel,
        out_shape=(
            jax.ShapeDtypeStruct((ROWS, COLS, 128), BF16),
            jax.ShapeDtypeStruct((128, 4, 128), F32),
            jax.ShapeDtypeStruct((8, 128), F32),
        ),
        in_specs=[vmem] * 6,
        out_specs=(vmem,) * 3,
        scratch_shapes=[
            pltpu.VMEM((16, 240, 256), BF16),
            pltpu.VMEM((4, 8, 2, 240, 256), BF16),
            pltpu.VMEM((2, OWNERS, 240, 128), BF16),
            pltpu.VMEM((2, OWNERS, 240, 128), BF16),
            pltpu.VMEM((2, 8, 240, 256), BF16),
            pltpu.VMEM((2, 4, 256, 256), BF16),
            pltpu.VMEM((CROP * 8, 128), F32),
            pltpu.VMEM((2, OWNERS, 240, 128), BF16),
            pltpu.VMEM((2, OWNERS, 240, 128), BF16),
            pltpu.VMEM((2 * PAIRS, 128, 256), F32),
            pltpu.VMEM((2 * PAIRS, 1, 256), F32),
            pltpu.VMEM((2 * PAIRS, 144, 256), BF16),
            pltpu.VMEM((128, 256), F32),
            pltpu.VMEM((128, 256), F32),
            pltpu.VMEM((512, 128), BF16),
            pltpu.VMEM((128, 512), BF16),
            pltpu.VMEM((512, 256), F32),
            pltpu.VMEM((128, 256), F32),
            pltpu.VMEM((128, 256), F32),
            pltpu.VMEM((512, 128), F32),
            pltpu.VMEM((512, 128), F32),
            pltpu.VMEM((144, 512), F32),
            pltpu.VMEM((8, 128), F32),
            pltpu.VMEM((OWNERS, 32, 128), BF16),
            pltpu.VMEM((OWNERS, 32, 128), BF16),
            pltpu.VMEM((4, 24, 128), F32),
            pltpu.VMEM((OWNERS, 16, 128), F32),
            dma((8,)), dma((8,)), dma((8, 2)), dma((8, 2)), dma((8, 2)), dma((8, 2)),
            dma((2, OWNERS)), dma((2, OWNERS)), dma((3, OWNERS)), dma((3, OWNERS)),
            dma((OWNERS,)), dma((OWNERS,)), dma((4,)), dma((4,)), dma((OWNERS,)), dma((OWNERS,)),
        ],
        compiler_params=pltpu.CompilerParams(
            collective_id=0, has_side_effects=True, vmem_limit_bytes=60 << 20
        ),
        name="triangle_backward",
    )(pair, prod_cot, proj_weight, proj_bias, norm_gain.reshape(1, 128), norm_shift.reshape(1, 128))
    return grad_pair, dw, small[0:4], small[4], small[5]


def solution(mesh):
    in_specs = (P(("row", "ch"), "col", None), P(), P(), P(), P(), P("ch", "row", "col"))
    out_specs = (P(("row", "ch"), "col", None), P(), P(), P(), P())
    return jax.shard_map(shards, mesh=mesh, in_specs=in_specs, out_specs=out_specs, check_vma=False)
```

```python
import functools

import jax
import jax.numpy as jnp
from jax import lax
from jax.experimental import pallas as pl
from jax.experimental.pallas import tpu as pltpu
from jax.sharding import PartitionSpec as P

MESH = pl.DeviceIdType.MESH
EPSILON = 1e-05
CROP = 960
ROWS = 30
COLS = 240
PAIRS = ROWS // 2
HALF_COLS = (128, COLS - 128)
OWNERS = 32
F32, BF16 = jnp.float32, jnp.bfloat16

STEPS = (
    (2, 2),
    (1, 1), (3, 3), (1, 3), (3, 1),
    (1, 2), (2, 1), (3, 2), (2, 3),
    (2, 0), (0, 2),
    (1, 0), (0, 1), (3, 0), (0, 3),
)
OFFSETS = [(dz, dy, core) for core in range(2) for dz, dy in STEPS] + [(0, 0, 1)]


LAST = 8
BACK_CHUNKS = ((0, 0, PAIRS), (1, 0, LAST), (1, LAST, PAIRS))
BACK = ((0,), (1, 2))
GROUPS = [(kind, t, side) for kind in range(2) for t in range(OWNERS) for side in range(2)]


def owner_row(kind, t, side):
    return kind * 256 + t * 8 + side * 4


def stream_row(kind, t, side):
    return (side * 2 + kind) * 128 + (t % 4) * 32 + (t // 4) * 4


def kernel(
    pair_hbm, cot_ref, weight_ref, biases_ref, gains_ref, shifts_ref,
    grad_hbm, dw_ref, bias_out, gain_out, shift_out,
    stage, cotf, send1, recv1, left, right, wide, send2, recv2, scaled_s, inv_s, normed_s, acc_gain, acc_shift,
    wt_ref, wb_ref, bias_ref, gain_ref, shift_ref, natural, owned, acc, small, part_s, part_r, line, whole,
    pair_ref, grad_ref, late, io,
    cs, cr, xs, xr, fs, fr, s1, r1, s2, r2, as_, ar, bs, br, gs_, gr,
):
    row, col, ch = lax.axis_index("row"), lax.axis_index("col"), lax.axis_index("ch")
    me = row * 4 + ch
    z = (ch // 2) * 2 + row // 4
    y = row % 4
    core = ch % 2
    east, west, far = (col + 1) % 4, (col + 3) % 4, (col + 2) % 4

    partners = []
    for dz, dy, dk in OFFSETS:
        z2, y2, k2 = (z + dz) % 4, (y + dy) % 4, (core + dk) % 2
        partners.append(((z2 % 2) * 4 + y2, (z2 // 2) * 2 + k2))

    load = pltpu.make_async_copy(pair_hbm, pair_ref, io.at[0])
    load.start()
    barrier = pltpu.get_barrier_semaphore()
    for r, g in partners:
        pl.semaphore_signal(barrier, 1, device_id=(r, col, g), device_id_type=MESH)
    for c in (east, west, far):
        pl.semaphore_signal(barrier, 1, device_id=(row, c, ch), device_id_type=MESH)

    def stage_one(pair, carry):
        stage[pair] = jnp.zeros((240, 256), BF16)
        stage[pair, 0:120, 0:COLS] = cot_ref[2 * pair]
        stage[pair, 120:240, 0:COLS] = cot_ref[2 * pair + 1]
        return carry

    lax.fori_loop(0, 16, stage_one, 0)
    pl.semaphore_wait(barrier, len(partners) + 3)

    def cot_copy(there):
        return pltpu.make_async_remote_copy(
            src_ref=stage.at[pl.ds(there * 2, 2)], dst_ref=cotf.at[col, row],
            send_sem=cs.at[there], recv_sem=cr.at[row],
            device_id=(there, col, ch), device_id_type=MESH,
        )

    def cot_arrival(source):
        return pltpu.make_async_remote_copy(
            src_ref=stage.at[pl.ds(source * 2, 2)], dst_ref=cotf.at[col, source],
            send_sem=cs.at[source], recv_sem=cr.at[source],
            device_id=(row, col, ch), device_id_type=MESH,
        )

    def x_copy(block, r, sems, recvs, side, there):
        return pltpu.make_async_remote_copy(
            src_ref=cotf.at[block, r], dst_ref=cotf.at[block, r],
            send_sem=sems.at[r, side], recv_sem=recvs.at[r, side],
            device_id=(row, there, ch), device_id_type=MESH,
        )

    def x_relay(block, r, side, there):
        return pltpu.make_async_remote_copy(
            src_ref=cotf.at[block, r, side], dst_ref=cotf.at[block, r, side],
            send_sem=fs.at[r, side], recv_sem=fr.at[r, side],
            device_id=(row, there, ch), device_id_type=MESH,
        )

    blocks = [row]
    for step in (6, 5, 7, 2, 4, 1, 3):
        z_lo = (row // 4 + step // 4) % 2
        cot_copy(z_lo * 4 + (row + step) % 4).start()
        blocks.append(z_lo * 4 + (row + 8 - step) % 4)
    cotf[col, row] = stage[pl.ds(row * 2, 2)]

    def x_send(n):
        r = blocks[n]
        if n > 0:
            cot_arrival(r).wait_recv()
        x_copy(col, r, xs, xr, 0, east).start()
        x_copy(col, r, xs, xr, 1, west).start()

    def x_forward(n):
        r = blocks[n]
        x_copy(west, r, xs, xr, 0, east).wait_recv()
        x_relay(west, r, 0, east).start()
        x_copy(east, r, xs, xr, 1, west).wait_recv()
        x_relay(east, r, 1, west).start()

    def x_finish(n):
        r = blocks[n]
        x_relay(far, r, 0, east).wait_recv()
        x_relay(far, r, 1, west).wait_recv()

    x_send(0)

    def to_owners():
        for kind, t, side in GROUPS:
            owned[owner_row(kind, t, side):owner_row(kind, t, side) + 4] = natural[
                stream_row(kind, t, side):stream_row(kind, t, side) + 4
            ]

    def to_streams():
        for kind, t, side in GROUPS:
            natural[stream_row(kind, t, side):stream_row(kind, t, side) + 4] = owned[
                owner_row(kind, t, side):owner_row(kind, t, side) + 4
            ]

    weights = weight_ref[...].astype(F32)
    for s in range(4):
        natural[s * 128:(s + 1) * 128] = weights[:, s, :].T
    to_owners()
    wt_ref[...] = owned[...].astype(BF16)
    for s in range(4):
        wb_ref[:, s * 128:(s + 1) * 128] = owned[s * 128:(s + 1) * 128].T.astype(BF16)
    for s in range(4):
        natural[s * 128:(s + 1) * 128] = jnp.broadcast_to(biases_ref[s:s + 1], (128, 128)).T
    to_owners()
    for half in range(2):
        lanes = slice(half * 128, (half + 1) * 128)
        bias_ref[:, lanes] = owned[...]
        gain_ref[:, lanes] = jnp.broadcast_to(gains_ref[...], (128, 128)).T
        shift_ref[:, lanes] = jnp.broadcast_to(shifts_ref[...], (128, 128)).T

    left[...] = jnp.zeros_like(left)
    for p in range(2):
        for x in range(4):
            right[p, x, COLS:256] = jnp.zeros((16, 256), BF16)
    acc[...] = jnp.zeros_like(acc)
    small[...] = jnp.zeros_like(small)
    acc_gain[...] = jnp.zeros_like(acc_gain)
    acc_shift[...] = jnp.zeros_like(acc_shift)

    def forward(kh, ip, carry):
        width = HALF_COLS[kh]
        tokens = []
        for half in range(2):
            x = pair_ref[2 * ip + half, kh * 128:kh * 128 + width].astype(F32)
            if width < 128:
                x = jnp.concatenate([x, jnp.zeros((128 - width, 128), F32)], axis=0)
            tokens.append(x.T)
        x = jnp.concatenate(tokens, axis=1)
        centred = x - jnp.mean(x, axis=0, keepdims=True)
        inv_std = lax.rsqrt(jnp.mean(centred * centred, axis=0, keepdims=True) + EPSILON)
        scaled = centred * inv_std
        normed = (scaled * gain_ref[...] + shift_ref[...]).astype(BF16)
        slot = kh * PAIRS + ip
        scaled_s[slot] = scaled
        inv_s[slot] = inv_std
        normed_s[slot, 0:128] = normed
        normed_s[slot, 128:144] = jnp.ones((16, 256), BF16)
        linear = jnp.dot(wt_ref[...], normed, preferred_element_type=F32) + bias_ref[...]
        gate = 0.5 * jnp.tanh(0.5 * linear[0:256]) + 0.5
        side = gate * linear[256:512]
        if width < 128:
            lane = lax.broadcasted_iota(jnp.int32, (256, 256), 1)
            side = jnp.where(lane % 128 < width, side, 0.0)
        packed = jnp.concatenate(
            [side[:, 0:128].reshape(OWNERS, 8, 128), side[:, 128:256].reshape(OWNERS, 8, 128)], axis=1
        ).astype(BF16)
        send1[kh, :, pl.ds(pl.multiple_of(ip * 16, 16), 16), :] = packed
        return carry

    def exchange(source, target, send_sem, recv_sem, kh, there_r, there_g):
        there = there_r * 4 + there_g
        return pltpu.make_async_remote_copy(
            src_ref=source.at[kh, there], dst_ref=target.at[kh, me],
            send_sem=send_sem.at[kh, there], recv_sem=recv_sem.at[kh, me],
            device_id=(there_r, col, there_g), device_id_type=MESH,
        )

    def arrival(source, target, send_sem, recv_sem, kh, there):
        return pltpu.make_async_remote_copy(
            src_ref=source.at[kh, there], dst_ref=target.at[kh, there],
            send_sem=send_sem.at[kh, there], recv_sem=recv_sem.at[kh, there],
            device_id=(row, col, ch), device_id_type=MESH,
        )

    def send_all(source, target, send_sem, recv_sem, kh):
        for r, g in partners:
            exchange(source, target, send_sem, recv_sem, kh, r, g).start()
        target[kh, me] = source[kh, me]

    def others(action):
        def one(there, carry):
            @pl.when(there != me)
            def _():
                action(there)
            return carry

        lax.fori_loop(0, OWNERS, one, 0)

    def regroup(kh):
        others(lambda there: arrival(send1, recv1, s1, r1, kh, there).wait_recv())

        def widen(source, carry):
            wide[pl.ds(pl.multiple_of(source * 240, 8), 240)] = recv1[kh, source].astype(F32)
            return carry

        lax.fori_loop(0, OWNERS, widen, 0)
        for p in range(2):
            for q in range(2):
                lanes = slice(q * 128, q * 128 + 128)
                for r in range(8):
                    left[p, r, q * 120:q * 120 + 120, lanes] = wide[
                        pl.ds(r * 960 + 2 * p + q, 120, stride=8)
                    ].astype(BF16)
                for x in range(4):
                    right[p, x, 0:COLS, lanes] = wide[
                        pl.ds(x * 1920 + 4 + 2 * p + q, COLS, stride=8)
                    ].astype(BF16)

    def triangle(group, first):
        for n in group:
            r = blocks[n]
            for p in range(2):
                total = jnp.dot(cotf[0, r, p], right[p, 0], preferred_element_type=F32)
                for x in range(1, 4):
                    total += jnp.dot(cotf[x, r, p], right[p, x], preferred_element_type=F32)
                for q in range(2):
                    wide[pl.ds(r * 960 + 2 * p + q, 120, stride=8)] = total[
                        q * 120:q * 120 + 120, q * 128:q * 128 + 128
                    ]
        for p in range(2):
            for x in range(4):
                total = None
                for n in group:
                    term = lax.dot_general(
                        cotf[x, blocks[n], p], left[p, blocks[n]], (((0,), (0,)), ((), ())),
                        preferred_element_type=F32,
                    )
                    total = term if total is None else total + term
                for q in range(2):
                    rows = pl.ds(x * 1920 + 4 + 2 * p + q, COLS, stride=8)
                    part = total[0:COLS, q * 128:q * 128 + 128]
                    wide[rows] = part if first else wide[rows] + part

    def give_back(kh):
        def narrow(target, carry):
            send2[kh, target] = wide[pl.ds(pl.multiple_of(target * 240, 8), 240)].astype(BF16)
            return carry

        lax.fori_loop(0, OWNERS, narrow, 0)
        for n in BACK[kh]:
            for r, g in partners:
                back_copy(n, r * 4 + g, me, r, g).start()
        recv2[kh, me] = send2[kh, me]

    def back_copy(n, source, target, r, g):
        kh, start, stop = BACK_CHUNKS[n]
        rows = pl.ds(start * 16, (stop - start) * 16)
        return pltpu.make_async_remote_copy(
            src_ref=send2.at[kh, source, rows], dst_ref=recv2.at[kh, target, rows],
            send_sem=s2.at[n, source], recv_sem=r2.at[n, target],
            device_id=(r, col, g), device_id_type=MESH,
        )

    def backward(kh, deferred, ip, carry):
        slot = kh * PAIRS + ip
        back = recv2[kh, :, pl.ds(pl.multiple_of(ip * 16, 16), 16), :].astype(F32)
        side_grad = jnp.concatenate(
            [back[:, 0:8].reshape(256, 128), back[:, 8:16].reshape(256, 128)], axis=1
        )
        normed = normed_s[slot, 0:128]
        linear = jnp.dot(wt_ref[...], normed, preferred_element_type=F32) + bias_ref[...]
        gate = 0.5 * jnp.tanh(0.5 * linear[0:256]) + 0.5
        value_grad = side_grad * gate
        gate_grad = value_grad * linear[256:512] * (1.0 - gate)
        linear_grad = jnp.concatenate([gate_grad.astype(BF16), value_grad.astype(BF16)], axis=0)
        normed_grad = jnp.dot(wb_ref[...], linear_grad, preferred_element_type=F32)
        acc[...] += lax.dot_general(
            normed_s[slot], linear_grad, (((1,), (1,)), ((), ())), preferred_element_type=F32
        )
        acc_gain[...] += normed_grad * scaled_s[slot]
        acc_shift[...] += normed_grad
        if deferred:
            late[ip - LAST] = normed_grad
        else:
            pair_gradient(kh, ip, normed_grad)
        return carry

    def pair_gradient(kh, ip, normed_grad):
        width = HALF_COLS[kh]
        slot = kh * PAIRS + ip
        scaled = scaled_s[slot]
        gained = normed_grad * gain_ref[...]
        centre = jnp.mean(gained, axis=0, keepdims=True)
        slope = jnp.mean(gained * scaled, axis=0, keepdims=True)
        result = (gained - centre - scaled * slope) * inv_s[slot]
        for half in range(2):
            out = result[:, half * 128:(half + 1) * 128].T.astype(BF16)
            grad_ref[2 * ip + half, kh * 128:kh * 128 + width] = out[0:width]

    def finish_late(ip, carry):
        pair_gradient(1, ip, late[ip - LAST])
        return carry

    load.wait()
    lax.fori_loop(0, 8, functools.partial(forward, 0), 0)
    x_send(1)
    lax.fori_loop(8, PAIRS, functools.partial(forward, 0), 0)
    send_all(send1, recv1, s1, r1, 0)
    x_send(2)
    x_forward(0)
    lax.fori_loop(0, 5, functools.partial(forward, 1), 0)
    x_send(3)
    x_forward(1)
    lax.fori_loop(5, 10, functools.partial(forward, 1), 0)
    x_send(4)
    x_forward(2)
    lax.fori_loop(10, PAIRS, functools.partial(forward, 1), 0)
    send_all(send1, recv1, s1, r1, 1)
    x_send(5)
    x_forward(3)
    x_send(6)
    x_forward(4)
    x_send(7)
    x_forward(5)
    regroup(0)
    x_forward(6)
    for n in range(6):
        x_finish(n)
    triangle(range(0, 6), True)
    x_forward(7)
    x_finish(6)
    x_finish(7)
    triangle(range(6, 8), False)
    give_back(0)
    regroup(1)
    triangle(range(0, 8), True)
    give_back(1)
    for n, (kh, start, stop) in enumerate(BACK_CHUNKS):
        others(lambda there: back_copy(n, there, there, row, ch).wait_recv())
        lax.fori_loop(start, stop, functools.partial(backward, kh, kh == 1 and start == LAST), 0)

    for s in range(4):
        small[s:s + 1] = acc[128:129, s * 128:(s + 1) * 128]
    small[4:5] = jnp.sum(acc_gain[...].T, axis=0, keepdims=True)
    small[5:6] = jnp.sum(acc_shift[...].T, axis=0, keepdims=True)
    coarse = small[...].astype(BF16)
    fine = small[...] - coarse.astype(F32)
    small_parts = jnp.concatenate([coarse.astype(F32), fine], axis=0).astype(BF16)
    for o in range(OWNERS):
        rows, lane = slice((o // 2) * 8, (o // 2) * 8 + 8), (o % 2) * 256
        part_s[o, 0:16] = jnp.concatenate(
            [acc[rows, lane:lane + 128], acc[rows, lane + 128:lane + 256]], axis=0
        ).astype(BF16)
        part_s[o, 16:32] = small_parts
    for r, g in partners:
        there = r * 4 + g
        pltpu.make_async_remote_copy(
            src_ref=part_s.at[there], dst_ref=part_r.at[me], send_sem=as_.at[there], recv_sem=ar.at[me],
            device_id=(r, col, g), device_id_type=MESH,
        ).start()
    part_r[me] = part_s[me]
    lax.fori_loop(LAST, PAIRS, finish_late, 0)
    store = pltpu.make_async_copy(grad_ref, grad_hbm, io.at[1])
    store.start()

    def part_arrival(there):
        return pltpu.make_async_remote_copy(
            src_ref=part_s.at[there], dst_ref=part_r.at[there], send_sem=as_.at[there], recv_sem=ar.at[there],
            device_id=(row, col, ch), device_id_type=MESH,
        )

    others(lambda there: part_arrival(there).wait_recv())
    total = part_r[0].astype(F32)
    for o in range(1, OWNERS):
        total = total + part_r[o].astype(F32)
    line[col, 0:16] = total[0:16]
    line[col, 16:24] = total[16:24] + total[24:32]

    def line_copy(slot, there):
        return pltpu.make_async_remote_copy(
            src_ref=line.at[slot], dst_ref=line.at[slot], send_sem=bs.at[there], recv_sem=br.at[slot],
            device_id=(row, there, ch), device_id_type=MESH,
        )

    for there in (far, east, west):
        line_copy(col, there).start()
    for there in (far, east, west):
        line_copy(there, there).wait_recv()
    total = (line[0] + line[1]) + (line[2] + line[3])
    total = total * (1.0 / CROP)
    whole[me] = total[0:16]
    small[...] = total[16:24]
    gain_out[...] = small[4:5]
    shift_out[...] = small[5:6]

    def whole_copy(slot, there, r, g):
        return pltpu.make_async_remote_copy(
            src_ref=whole.at[slot], dst_ref=whole.at[slot], send_sem=gs_.at[there], recv_sem=gr.at[slot],
            device_id=(r, col, g), device_id_type=MESH,
        )

    for r, g in partners:
        whole_copy(me, r * 4 + g, r, g).start()
    others(lambda there: whole_copy(there, there, row, ch).wait_recv())
    for o in range(OWNERS):
        rows, lane = slice((o // 2) * 8, (o // 2) * 8 + 8), (o % 2) * 256
        acc[rows, lane:lane + 128] = whole[o, 0:8]
        acc[rows, lane + 128:lane + 256] = whole[o, 8:16]
    for s in range(4):
        owned[s * 128:(s + 1) * 128] = acc[0:128, s * 128:(s + 1) * 128].T
    to_streams()
    for s in range(4):
        dw_ref[:, s, :] = natural[s * 128:(s + 1) * 128].T
    for s in range(4):
        owned[s * 128:(s + 1) * 128] = jnp.broadcast_to(small[s:s + 1], (128, 128)).T
    to_streams()
    for s in range(4):
        bias_out[s:s + 1] = natural[s * 128:(s + 1) * 128].T[0:1]

    store.wait()
    others(lambda there: part_arrival(there).wait_send())
    others(lambda there: whole_copy(me, there, row, ch).wait_send())
    for there in (far, east, west):
        line_copy(col, there).wait_send()
    for n in range(8):
        r = blocks[n]
        if n > 0:
            cot_copy(r).wait_send()
        x_copy(col, r, xs, xr, 0, east).wait_send()
        x_copy(col, r, xs, xr, 1, west).wait_send()
        x_relay(west, r, 0, east).wait_send()
        x_relay(east, r, 1, west).wait_send()
    for kh in range(2):
        others(lambda there: arrival(send1, recv1, s1, r1, kh, there).wait_send())
    for n in range(len(BACK_CHUNKS)):
        others(lambda there: back_copy(n, there, there, row, ch).wait_send())


def shards(pair, norm_gain, norm_shift, proj_weight, proj_bias, prod_cot):
    vmem = pl.BlockSpec(memory_space=pltpu.VMEM)
    dma = pltpu.SemaphoreType.DMA
    grad_pair, dw, bias, gain, shift = pl.pallas_call(
        kernel,
        out_shape=(
            jax.ShapeDtypeStruct((ROWS, COLS, 128), BF16),
            jax.ShapeDtypeStruct((128, 4, 128), F32),
            jax.ShapeDtypeStruct((4, 128), F32),
            jax.ShapeDtypeStruct((1, 128), F32),
            jax.ShapeDtypeStruct((1, 128), F32),
        ),
        in_specs=[pl.BlockSpec(memory_space=pl.ANY)] + [vmem] * 5,
        out_specs=(pl.BlockSpec(memory_space=pl.ANY),) + (vmem,) * 4,
        scratch_shapes=[
            pltpu.VMEM((16, 240, 256), BF16),
            pltpu.VMEM((4, 8, 2, 240, 256), BF16),
            pltpu.VMEM((2, OWNERS, 240, 128), BF16),
            pltpu.VMEM((2, OWNERS, 240, 128), BF16),
            pltpu.VMEM((2, 8, 240, 256), BF16),
            pltpu.VMEM((2, 4, 256, 256), BF16),
            pltpu.VMEM((CROP * 8, 128), F32),
            pltpu.VMEM((2, OWNERS, 240, 128), BF16),
            pltpu.VMEM((2, OWNERS, 240, 128), BF16),
            pltpu.VMEM((2 * PAIRS, 128, 256), F32),
            pltpu.VMEM((2 * PAIRS, 1, 256), F32),
            pltpu.VMEM((2 * PAIRS, 144, 256), BF16),
            pltpu.VMEM((128, 256), F32),
            pltpu.VMEM((128, 256), F32),
            pltpu.VMEM((512, 128), BF16),
            pltpu.VMEM((128, 512), BF16),
            pltpu.VMEM((512, 256), F32),
            pltpu.VMEM((128, 256), F32),
            pltpu.VMEM((128, 256), F32),
            pltpu.VMEM((512, 128), F32),
            pltpu.VMEM((512, 128), F32),
            pltpu.VMEM((144, 512), F32),
            pltpu.VMEM((8, 128), F32),
            pltpu.VMEM((OWNERS, 32, 128), BF16),
            pltpu.VMEM((OWNERS, 32, 128), BF16),
            pltpu.VMEM((4, 24, 128), F32),
            pltpu.VMEM((OWNERS, 16, 128), F32),
            pltpu.VMEM((ROWS, COLS, 128), BF16),
            pltpu.VMEM((ROWS, COLS, 128), BF16),
            pltpu.VMEM((PAIRS - LAST, 128, 256), F32),
            dma((2,)),
            dma((8,)), dma((8,)), dma((8, 2)), dma((8, 2)), dma((8, 2)), dma((8, 2)),
            dma((2, OWNERS)), dma((2, OWNERS)), dma((3, OWNERS)), dma((3, OWNERS)),
            dma((OWNERS,)), dma((OWNERS,)), dma((4,)), dma((4,)), dma((OWNERS,)), dma((OWNERS,)),
        ],
        compiler_params=pltpu.CompilerParams(
            collective_id=0, has_side_effects=True, vmem_limit_bytes=60 << 20
        ),
        name="triangle_backward",
    )(pair, prod_cot, proj_weight, proj_bias, norm_gain.reshape(1, 128), norm_shift.reshape(1, 128))
    return grad_pair, dw, bias, gain.reshape(128), shift.reshape(128)


def solution(mesh):
    in_specs = (P(("row", "ch"), "col", None), P(), P(), P(), P(), P("ch", "row", "col"))
    out_specs = (P(("row", "ch"), "col", None), P(), P(), P(), P())
    return jax.shard_map(shards, mesh=mesh, in_specs=in_specs, out_specs=out_specs, check_vma=False)
```
